128 devices in a mesh: pa: 32 (over y_lo, x, z), pb: 4 (over y_hi, core).
Axes of the slice: x: 4, y: 4 (y_hi: 2, y_lo: 2; y = y_hi * 2 + y_lo), z: 4, core: 2. Of those that a mesh axis runs over, the one named last changes fastest.
Arguments:
- particles: bfloat16 [98304, 1024], P(('pa', 'pb')), may hold values from -7 to 7
- scores: bfloat16 [98304, 1024], P(('pa', 'pb')), may hold values from -5 to 5
- spread: float32 [1], replicated, may hold values from 256 to 341
- plan: int32 [2, 32], replicated, may hold values from 0 to 31, as said below
Outputs:
- drive: float32 [98304, 1024], P(('pa', 'pb'))
The draws below stay inside these ranges and needn't reach their ends.
Inputs may be any that keep to these rules, and one draw needn't show every extreme that they name: `plan`: row r lists, for each pa index a, the partner a XOR m_r, where m_r is a round mask of 1 to 31 and different rows have different masks.
All inputs are finite; a program needn't handle non-finite values.
Results may differ from the reference program's by a relative error of at most 0.00033.
Values may be sent and summed in bfloat16 or wider, within the bound.
No kernel may reach another device: no remote copies, remote signals or barrier semaphores. Data moves between devices by JAX's collectives and lax.ppermute only.
A program may use at most 128 MiB of HBM per device.

```python
import math
import jax
import jax.numpy as jnp
from jax import lax

K = 1024
TILE = 768
ROUNDS = 2
NP = 98304
N_PA = 32
N_PB = 4


def column_scales(key, low_exp, high_exp):
    exponents = jax.random.uniform(key, (K,), jnp.float32, low_exp, high_exp)
    mean_square = (jnp.exp(2.0 * high_exp) - jnp.exp(2.0 * low_exp)) / (2.0 * (high_exp - low_exp))
    return jnp.exp(exponents) / jnp.sqrt(mean_square)


def draw_particles(key, part):
    key = jax.random.fold_in(key, 11)
    scale_key, value_key = jax.random.split(key)
    scales = column_scales(scale_key, -1.151, 1.151)
    values = jax.random.truncated_normal(value_key, -3.0, 3.0, (NP, K), jnp.float32)
    return (values * scales[None, :]).astype(jnp.bfloat16)


def draw_scores(key, part):
    key = jax.random.fold_in(key, 13)
    common_key, noise_key = jax.random.split(key)
    common = 0.7 * jax.random.truncated_normal(common_key, -3.0, 3.0, (K,), jnp.float32)
    noise = 0.7 * jax.random.truncated_normal(noise_key, -3.0, 3.0, (NP, K), jnp.float32)
    return (common[None, :] + noise).astype(jnp.bfloat16)


def draw_plan(key, part):
    key = jax.random.fold_in(key, 7)
    masks = jax.random.permutation(key, N_PA - 1)[:ROUNDS].astype(jnp.int32) + 1
    lanes = jnp.arange(N_PA, dtype=jnp.int32)
    return jnp.bitwise_xor(lanes[None, :], masks[:, None]).astype(jnp.int32)


def setup_inputs(seed: int = 0) -> dict:
    splits = jax.random.split(jax.random.key(seed), 5)
    return {
        "particles": draw_particles(jax.random.fold_in(splits[4], 71), 0),
        "scores": draw_scores(jax.random.fold_in(splits[4], 71), 0),
        "spread": jnp.clip(jnp.exp(jax.random.uniform(splits[2], (1,), jnp.float32, math.log(256.0), math.log(341.0))), 256.0, 341.0),
        "plan": draw_plan(jax.random.fold_in(splits[4], 71), 0),
    }


def block_terms(row_parts, col_parts, col_drift, band_width):
    row_square = jnp.sum(jnp.square(row_parts.astype(jnp.float32)), axis=1)
    col_square = jnp.sum(jnp.square(col_parts.astype(jnp.float32)), axis=1)
    products = jnp.einsum("ik,jk->ij", row_parts, col_parts, preferred_element_type=jnp.float32)
    distance = row_square[:, None] + col_square[None, :] - 2.0 * products
    kernel = jnp.exp(-distance / band_width)
    pulled = jnp.dot(kernel.astype(jnp.bfloat16), col_drift, preferred_element_type=jnp.float32)
    return pulled, jnp.sum(kernel, axis=1)


def reference(particles, scores, spread, plan):
    band_width = spread[0]
    float_rows = particles.astype(jnp.float32)
    drift_rows = (scores.astype(jnp.float32) - (2.0 / band_width) * float_rows).astype(jnp.bfloat16)
    particle_grid = particles.reshape(N_PA, N_PB, TILE, K)
    drift_grid = drift_rows.reshape(N_PA, N_PB, TILE, K)

    def per_group(group):
        group_rows = lax.dynamic_index_in_dim(particle_grid, group, 0, keepdims=False)
        group_drift = lax.dynamic_index_in_dim(drift_grid, group, 0, keepdims=False)
        flat_rows = group_rows.reshape(N_PB * TILE, K)
        pulled, row_total = block_terms(flat_rows, flat_rows, group_drift.reshape(N_PB * TILE, K), band_width)
        pulled = pulled.reshape(N_PB, TILE, K)
        row_total = row_total.reshape(N_PB, TILE)
        for round_no in range(ROUNDS):
            partner = plan[round_no][group].astype(jnp.int32)
            partner_rows = lax.dynamic_index_in_dim(particle_grid, partner, 0, keepdims=False)
            partner_drift = lax.dynamic_index_in_dim(drift_grid, partner, 0, keepdims=False)
            extra_pull, extra_total = jax.vmap(block_terms, in_axes=(0, 0, 0, None))(group_rows, partner_rows, partner_drift, band_width)
            pulled = pulled + extra_pull
            row_total = row_total + extra_total
        return pulled + (2.0 / band_width) * group_rows.astype(jnp.float32) * row_total[:, :, None]

    result = lax.map(per_group, jnp.arange(N_PA, dtype=jnp.int32))
    return result.reshape(NP, K)
```

```python
import functools

import jax
import jax.numpy as jnp
import numpy as np
from jax import lax
from jax.experimental import pallas as pl
from jax.experimental.pallas import tpu as pltpu
from jax.sharding import PartitionSpec as P

STEP = 256
Y_NEXT = 16
PLANE = 16


def absorb_kernel(count, first, last, h_ref, own_ref, *refs):
    parts, scores = refs[:count], refs[count : 2 * count]
    refs = refs[2 * count :]
    if not first:
        sum_in, total_in = refs[:2]
        refs = refs[2:]
    out_ref = refs[0]
    refs = refs[1:]
    if not last:
        total_out = refs[0]
        refs = refs[1:]
    x_buf, d_buf, own_square, col_square, total, sems = refs
    rows, knots = own_ref.shape
    steps = rows // STEP
    scale = 2.0 / h_ref[0]
    rate = -1.0 / h_ref[0]

    def copies(b):
        return (
            pltpu.make_async_copy(parts[b], x_buf.at[b], sems.at[b, 0]),
            pltpu.make_async_copy(scores[b], d_buf.at[b], sems.at[b, 1]),
        )

    for b in range(count):
        for copy in copies(b):
            copy.start()

    def prepare(t, carry):
        at = pl.ds(pl.multiple_of(t * STEP, STEP), STEP)
        mine = own_ref[at, :].astype(jnp.float32)
        own_square[at, :] = jnp.broadcast_to(
            jnp.sum(mine * mine, axis=1, keepdims=True), (STEP, 128)
        )
        if first:
            out_ref[at, :] = jnp.zeros((STEP, knots), jnp.float32)
            total[at, :] = jnp.zeros((STEP, 128), jnp.float32)
        else:
            out_ref[at, :] = sum_in[at, :]
            total[at, :] = total_in[at, :]
        return carry

    lax.fori_loop(0, steps, prepare, 0)

    for b in range(count):
        for copy in copies(b):
            copy.wait()

    def one_block(b, carry):
        def columns(t, carry):
            at = pl.ds(pl.multiple_of(t * STEP, STEP), STEP)
            x = x_buf[b, at, :].astype(jnp.float32)
            d = d_buf[b, at, :].astype(jnp.float32) - scale * x
            d_buf[b, at, :] = d.astype(jnp.bfloat16)
            square = x * x
            high = square.astype(jnp.bfloat16)
            low = (square - high.astype(jnp.float32)).astype(jnp.bfloat16)
            ones = jnp.ones((8, knots), jnp.bfloat16)
            dims = (((1,), (1,)), ((), ()))
            col_square[:, at] = lax.dot_general(
                ones, high, dims, preferred_element_type=jnp.float32
            ) + lax.dot_general(ones, low, dims, preferred_element_type=jnp.float32)
            return carry

        lax.fori_loop(0, steps, columns, 0)

        def tile(t, carry):
            at = pl.ds(pl.multiple_of(t * STEP, STEP), STEP)
            products = lax.dot_general(
                own_ref[at, :],
                x_buf[b],
                (((1,), (1,)), ((), ())),
                preferred_element_type=jnp.float32,
            )
            distance = own_square[at, :1] + col_square[:1, :] - 2.0 * products
            kernel = jnp.exp(distance * rate)
            total[at, :] += jnp.broadcast_to(jnp.sum(kernel, axis=1, keepdims=True), (STEP, 128))
            out_ref[at, :] += jnp.dot(
                kernel.astype(jnp.bfloat16), d_buf[b], preferred_element_type=jnp.float32
            )
            return carry

        lax.fori_loop(0, steps, tile, 0)
        return carry

    lax.fori_loop(0, count, one_block, 0)

    def finish(t, carry):
        at = pl.ds(pl.multiple_of(t * STEP, STEP), STEP)
        if last:
            mine = own_ref[at, :].astype(jnp.float32)
            out_ref[at, :] += scale * mine * total[at, :1]
        else:
            total_out[at, :] = total[at, :]
        return carry

    lax.fori_loop(0, steps, finish, 0)


def absorb(spread, own, blocks, running, last):
    rows, knots = own.shape
    count, first = len(blocks), running is None
    vmem = pl.BlockSpec(memory_space=pltpu.VMEM)
    anywhere = pl.BlockSpec(memory_space=pl.ANY)
    out_shape = [jax.ShapeDtypeStruct((rows, knots), jnp.float32)]
    if not last:
        out_shape.append(jax.ShapeDtypeStruct((rows, 128), jnp.float32))
    return pl.pallas_call(
        functools.partial(absorb_kernel, count, first, last),
        out_shape=out_shape,
        in_specs=[pl.BlockSpec(memory_space=pltpu.SMEM), vmem]
        + [anywhere] * (2 * count)
        + ([] if first else [vmem, vmem]),
        out_specs=[vmem] * len(out_shape),
        scratch_shapes=[
            pltpu.VMEM((count, rows, knots), jnp.bfloat16),
            pltpu.VMEM((count, rows, knots), jnp.bfloat16),
            pltpu.VMEM((rows, 128), jnp.float32),
            pltpu.VMEM((8, rows), jnp.float32),
            pltpu.VMEM((rows, 128), jnp.float32),
            pltpu.SemaphoreType.DMA((count, 2)),
        ],
        cost_estimate=pl.CostEstimate(
            flops=4 * count * rows * rows * knots,
            bytes_accessed=4 * (count + 2) * rows * knots,
            transcendentals=count * rows * rows,
        ),
        compiler_params=pltpu.CompilerParams(vmem_limit_bytes=48 * 1024 * 1024),
    )(spread, own, *[b[0] for b in blocks], *[b[1] for b in blocks], *(running or ()))


GRAY = [0, 1, 3, 2]
CODE_TO_MOVE = [GRAY.index(c >> 2) * 4 + GRAY.index(c & 3) for c in range(PLANE)]


def to_code(move):
    return move ^ (move >> 1 & 5)


def hop(block, move, pb_move=0):
    bits = move * lax.axis_size("pb") + pb_move
    if bits == 0:
        return block
    count = lax.axis_size(("pa", "pb"))
    return lax.ppermute(block, ("pa", "pb"), [(i, i ^ bits) for i in range(count)])


def subsets(free):
    return [c for c in range(PLANE) if c & ~free == 0]


def side_by_side(first, first_code, second, second_code, second_y):
    rank = np.zeros((PLANE, PLANE), np.int32)
    branches = []
    for code in range(PLANE):
        options = subsets(PLANE - 1 - code)
        for place, option in enumerate(options):
            rank[code, option] = place

        def branch(a, b, inner, code=code, options=options):
            moved = hop(a, CODE_TO_MOVE[code])
            if second_y is None:
                moves = [CODE_TO_MOVE[c] for c in options]
            else:
                moves = [CODE_TO_MOVE[c] + y for c in options for y in (0, Y_NEXT)]
            return moved, lax.switch(
                inner, [functools.partial(hop, move=move) for move in moves], b
            )

        branches.append(branch)
    inner = jnp.asarray(rank)[first_code, second_code]
    if second_y is not None:
        inner = 2 * inner + second_y
    return lax.switch(first_code, branches, first, second, inner)


def per_device(particles, scores, spread, plan):
    masks = plan[:, 0]
    swap = masks[0] >= Y_NEXT
    low = jnp.where(swap, masks[1], masks[0])
    high = jnp.where(swap, masks[0], masks[1])
    low_y, high_y = low // Y_NEXT, high // Y_NEXT
    low_code, high_code = to_code(low % Y_NEXT), to_code(high % Y_NEXT)
    shared = low_code & high_code
    both_y = low_y * high_y

    mate = (hop(particles, 0, 1), hop(scores, 0, 1))
    base = lax.cond(both_y == 1, functools.partial(hop, move=Y_NEXT), lambda x: x, particles)
    scores_y = hop(scores, Y_NEXT)
    part_way = lax.switch(
        shared, [functools.partial(hop, move=CODE_TO_MOVE[c]) for c in range(PLANE)], base
    )
    scores_far = hop(scores_y, Y_NEXT, 2)
    low_scores, high_parts = side_by_side(
        jnp.where(low_y == 1, scores_y, scores),
        low_code,
        part_way,
        high_code & ~shared,
        high_y - both_y,
    )
    late_particles, high_parts = lax.optimization_barrier((particles, high_parts))
    parts_far = hop(late_particles, 0, 2)
    high_scores, low_parts = side_by_side(
        jnp.where(high_y == 1, scores_y, scores), high_code, part_way, low_code & ~shared, None
    )
    running = absorb(spread, particles, [(particles, scores), mate], None, False)
    far = (parts_far, scores_far)
    far_mate = (hop(parts_far, 0, 1), hop(scores_far, 0, 1))
    return absorb(
        spread,
        particles,
        [(low_parts, low_scores), (high_parts, high_scores), far, far_mate],
        running,
        True,
    )[0]


def solution(mesh):
    in_specs = (P(("pa", "pb"), None), P(("pa", "pb"), None), P(), P())
    out_specs = P(("pa", "pb"), None)
    return jax.shard_map(
        per_device, mesh=mesh, in_specs=in_specs, out_specs=out_specs, check_vma=False
    )
```

```python
import functools

import jax
import jax.numpy as jnp
from jax import lax
from jax.experimental import pallas as pl
from jax.experimental.pallas import tpu as pltpu
from jax.sharding import PartitionSpec as P

LOG2E = 1.4426950408889634
Y_NEXT = 16
PLANE = 16
PRODUCT = (((1,), (1,)), ((), ()))


def fold(square):
    total = square[:, :128]
    for i in range(128, square.shape[1], 128):
        total = total + square[:, i : i + 128]
    return total


def prepare_rows(own_ref, own_square, rate, step, also=None):
    def rows(t, carry):
        at = pl.ds(pl.multiple_of(t * step, step), step)
        mine = own_ref[at, :].astype(jnp.float32)
        square = jnp.sum(fold(mine * mine), axis=1, keepdims=True) * rate
        own_square[at, :] = jnp.broadcast_to(square, (step, 128))
        if also is not None:
            also(at)
        return carry

    lax.fori_loop(0, own_ref.shape[0] // step, rows, 0)


def near_kernel(count, h_ref, own_ref, *refs):
    parts, scores = refs[:count], refs[count : 2 * count]
    out_ref, total, x_buf, d_buf, own_square, col_square, sems = refs[2 * count :]
    rows, knots = own_ref.shape
    scale, rate = 2.0 / h_ref[0], LOG2E / h_ref[0]
    step, tile = 32, 256

    def copies(b):
        return (
            pltpu.make_async_copy(parts[b], x_buf.at[b], sems.at[b, 0]),
            pltpu.make_async_copy(scores[b], d_buf.at[b], sems.at[b, 1]),
        )

    for b in range(count):
        for copy in copies(b):
            copy.start()

    def clear(at):
        out_ref[at, :] = jnp.zeros((step, knots), jnp.float32)
        total[at, :] = jnp.zeros((step, 128), jnp.float32)

    prepare_rows(own_ref, own_square, rate, step, clear)
    for b in range(count):
        for copy in copies(b):
            copy.wait()

    def block(b, carry):
        def columns(t, carry):
            squares = []
            for u in range(0, 128, step):
                at = pl.ds(pl.multiple_of(t * 128 + u, step), step)
                x = x_buf[b, at, :].astype(jnp.float32)
                d = d_buf[b, at, :].astype(jnp.float32) - scale * x
                d_buf[b, at, :] = d.astype(jnp.bfloat16)
                squares.append(fold(x * x))
            square = jnp.sum(jnp.transpose(jnp.concatenate(squares, axis=0)), axis=0, keepdims=True)
            at = pl.ds(pl.multiple_of(t * 128, 128), 128)
            col_square[:, at] = jnp.broadcast_to(square * rate, (8, 128))
            return carry

        lax.fori_loop(0, rows // 128, columns, 0)

        def one(t, carry):
            at = pl.ds(pl.multiple_of(t // (rows // tile) * tile, tile), tile)
            to = pl.ds(pl.multiple_of(t % (rows // tile) * tile, tile), tile)
            products = lax.dot_general(
                own_ref[at, :], x_buf[b, to, :], PRODUCT, preferred_element_type=jnp.float32
            )
            mine = jnp.concatenate([own_square[at, :]] * (tile // 128), axis=1)
            kernel = jnp.exp2(products * (2.0 * rate) - (mine + col_square[:1, to]))
            total[at, :] += fold(kernel)
            out_ref[at, :] += jnp.dot(
                kernel.astype(jnp.bfloat16), d_buf[b, to, :], preferred_element_type=jnp.float32
            )
            return carry

        lax.fori_loop(0, (rows // tile) ** 2, one, 0)
        return carry

    lax.fori_loop(0, count, block, 0)


def far_kernel(count, choice, last, h_ref, flag_ref, own_ref, *refs):
    names = count if choice is None else count + 1
    parts, scores = refs[:names], refs[names : names + count]
    sum_in, total_in, out_ref = refs[names + count : names + count + 3]
    refs = refs[names + count + 3 :]
    if not last:
        total_out = refs[0]
        refs = refs[1:]
    x_buf, s_buf, own_square, total, sems, sum_sems = refs
    rows, knots = own_ref.shape
    scale, rate = 2.0 / h_ref[0], LOG2E / h_ref[0]

    def part_copy(b, source):
        return pltpu.make_async_copy(source, x_buf.at[b], sems.at[b, 0])

    def score_copy(b):
        return pltpu.make_async_copy(scores[b], s_buf.at[b], sems.at[b, 1])

    sums = (
        pltpu.make_async_copy(sum_in, out_ref, sum_sems.at[0]),
        pltpu.make_async_copy(total_in, total, sum_sems.at[1]),
    )
    for b in range(count):
        if b == choice:
            pl.when(flag_ref[0] == 0)(lambda: part_copy(b, parts[b]).start())
            pl.when(flag_ref[0] != 0)(lambda: part_copy(b, parts[count]).start())
        else:
            part_copy(b, parts[b]).start()
        score_copy(b).start()
        if b == 0:
            for copy in sums:
                copy.start()

    prepare_rows(own_ref, own_square, rate, 256)
    for copy in sums:
        copy.wait()

    def block(b, carry):
        part_copy(b, parts[0]).wait()
        pltpu.make_async_copy(scores[0], s_buf.at[b], sems.at[b, 1]).wait()
        x = x_buf[b].astype(jnp.float32)
        drift = (s_buf[b].astype(jnp.float32) - scale * x).astype(jnp.bfloat16)
        square = jnp.sum(jnp.transpose(fold(x * x)), axis=0, keepdims=True) * rate
        products = lax.dot_general(
            own_ref[...], x_buf[b], PRODUCT, preferred_element_type=jnp.float32
        )
        mine = jnp.concatenate([own_square[...]] * (rows // 128), axis=1)
        kernel = jnp.exp2(products * (2.0 * rate) - (mine + square))
        total[...] += fold(kernel)
        out_ref[...] += jnp.dot(
            kernel.astype(jnp.bfloat16), drift, preferred_element_type=jnp.float32
        )
        return carry

    lax.fori_loop(0, count, block, 0)

    def finish(t, carry):
        at = pl.ds(pl.multiple_of(t * 256, 256), 256)
        if last:
            mine = own_ref[at, :].astype(jnp.float32)
            out_ref[at, :] += scale * mine * jnp.sum(total[at, :], axis=1, keepdims=True)
        else:
            total_out[at, :] = total[at, :]
        return carry

    lax.fori_loop(0, rows // 256, finish, 0)


SMEM = pl.BlockSpec(memory_space=pltpu.SMEM)
VMEM = pl.BlockSpec(memory_space=pltpu.VMEM)
ANY = pl.BlockSpec(memory_space=pl.ANY)


def common(count, rows, knots, call_blocks):
    return dict(
        cost_estimate=pl.CostEstimate(
            flops=4 * count * rows * rows * knots,
            bytes_accessed=4 * (count + 2) * rows * knots,
            transcendentals=count * rows * rows,
        ),
        compiler_params=pltpu.CompilerParams(vmem_limit_bytes=call_blocks * 1024 * 1024),
    )


def near_terms(spread, own, blocks):
    rows, knots = own.shape
    count = len(blocks)
    return pl.pallas_call(
        functools.partial(near_kernel, count),
        out_shape=[
            jax.ShapeDtypeStruct((rows, knots), jnp.float32),
            jax.ShapeDtypeStruct((rows, 128), jnp.float32),
        ],
        in_specs=[SMEM, VMEM] + [ANY] * (2 * count),
        out_specs=[VMEM, VMEM],
        scratch_shapes=[
            pltpu.VMEM((count, rows, knots), jnp.bfloat16),
            pltpu.VMEM((count, rows, knots), jnp.bfloat16),
            pltpu.VMEM((rows, 128), jnp.float32),
            pltpu.VMEM((8, rows), jnp.float32),
            pltpu.SemaphoreType.DMA((count, 2)),
        ],
        **common(count, rows, knots, 32),
    )(spread, own, *[b[0] for b in blocks], *[b[1] for b in blocks])


def far_terms(spread, flag, own, blocks, running, last, choice=None, other=None):
    rows, knots = own.shape
    count = len(blocks)
    parts = [b[0] for b in blocks] + ([] if choice is None else [other])
    out_shape = [jax.ShapeDtypeStruct((rows, knots), jnp.float32)]
    if not last:
        out_shape.append(jax.ShapeDtypeStruct((rows, 128), jnp.float32))
    return pl.pallas_call(
        functools.partial(far_kernel, count, choice, last),
        out_shape=out_shape,
        in_specs=[SMEM, SMEM, VMEM] + [ANY] * (len(parts) + count + 2),
        out_specs=[VMEM] * len(out_shape),
        scratch_shapes=[
            pltpu.VMEM((count, rows, knots), jnp.bfloat16),
            pltpu.VMEM((count, rows, knots), jnp.bfloat16),
            pltpu.VMEM((rows, 128), jnp.float32),
            pltpu.VMEM((rows, 128), jnp.float32),
            pltpu.SemaphoreType.DMA((count, 2)),
            pltpu.SemaphoreType.DMA((2,)),
        ],
        **common(count, rows, knots, 48),
    )(spread, flag, own, *parts, *[b[1] for b in blocks], *running)


GRAY = [0, 1, 3, 2]
CODE_TO_MOVE = [GRAY.index(c >> 2) * 4 + GRAY.index(c & 3) for c in range(PLANE)]


def to_code(move):
    return move ^ (move >> 1 & 5)


def hop(block, move, pb_move=0):
    bits = move * lax.axis_size("pb") + pb_move
    if bits == 0:
        return block
    count = lax.axis_size(("pa", "pb"))
    return lax.ppermute(block, ("pa", "pb"), [(i, i ^ bits) for i in range(count)])


def rank(option, free):
    place, value = 0, 0
    for k in range(4):
        value = value | (option >> k & 1) << place
        place = place + (free >> k & 1)
    return value


def side_by_side(first, first_code, second, second_code):
    branches = []
    for code in range(PLANE):
        moves = [CODE_TO_MOVE[c] for c in range(PLANE) if c & code == 0]

        def branch(a, b, inner, code=code, moves=moves):
            moved = hop(a, CODE_TO_MOVE[code])
            return moved, lax.switch(
                inner, [functools.partial(hop, move=move) for move in moves], b
            )

        branches.append(branch)
    inner = rank(second_code, first_code ^ (PLANE - 1))
    return lax.switch(first_code, branches, first, second, inner)


def per_device(particles, scores, spread, plan):
    masks = plan[:, 0]
    low, high = jnp.minimum(masks[0], masks[1]), jnp.maximum(masks[0], masks[1])
    low_y, high_y = low >> 4, high >> 4
    low_code, high_code = to_code(low & 15), to_code(high & 15)
    shared = low_code & high_code

    scores_y = hop(scores, Y_NEXT)
    mate = (hop(particles, 0, 1), hop(scores, 0, 1))
    base = lax.cond(low_y == 1, functools.partial(hop, move=Y_NEXT), lambda x: x, particles)

    def first_slot(move, base, spread, particles, scores, *mate):
        near = near_terms(spread, particles, [(particles, scores), mate])
        return hop(base, move), near

    part_way, running = lax.switch(
        shared,
        [functools.partial(first_slot, CODE_TO_MOVE[c]) for c in range(PLANE)],
        *(base, spread, particles, scores, *mate),
    )

    late_particles, part_way = lax.optimization_barrier((particles, part_way))
    parts_far = hop(late_particles, 0, 2)
    low_scores, high_parts = side_by_side(
        jnp.where(low_y == 1, scores_y, scores), low_code, part_way, high_code & ~shared
    )

    late_scores, part_way, high_parts, parts_far = lax.optimization_barrier(
        (scores_y, part_way, high_parts, parts_far)
    )
    scores_far = hop(late_scores, Y_NEXT, 2)
    high_parts_y = hop(high_parts, Y_NEXT)
    parts_far_mate = hop(parts_far, 0, 1)
    high_scores, low_parts = side_by_side(
        jnp.where(high_y == 1, scores_y, scores), high_code, part_way, low_code & ~shared
    )

    flag = (high_y & ~low_y).reshape(1)
    scores_far, low_parts = lax.optimization_barrier((scores_far, low_parts))
    scores_far_mate = hop(scores_far, 0, 1)
    running = far_terms(
        spread,
        flag,
        particles,
        [(low_parts, low_scores), (high_parts, high_scores), (parts_far, scores_far)],
        running,
        last=False,
        choice=1,
        other=high_parts_y,
    )
    return far_terms(
        spread, flag, particles, [(parts_far_mate, scores_far_mate)], running, last=True
    )[0]


def solution(mesh):
    in_specs = (P(("pa", "pb"), None), P(("pa", "pb"), None), P(), P())
    out_specs = P(("pa", "pb"), None)
    return jax.shard_map(
        per_device, mesh=mesh, in_specs=in_specs, out_specs=out_specs, check_vma=False
    )
```

```python
import functools

import jax
import jax.numpy as jnp
from jax import lax
from jax.experimental import pallas as pl
from jax.experimental.pallas import tpu as pltpu
from jax.sharding import PartitionSpec as P

LOG2E = 1.4426950408889634
Y_NEXT = 16
PLANE = 16
PRODUCT = (((1,), (1,)), ((), ()))


def fold(square):
    total = square[:, :128]
    for i in range(128, square.shape[1], 128):
        total = total + square[:, i : i + 128]
    return total


def prepare_rows(own_ref, own_square, rate, step, also=None):
    def rows(t, carry):
        at = pl.ds(pl.multiple_of(t * step, step), step)
        mine = own_ref[at, :].astype(jnp.float32)
        square = jnp.sum(fold(mine * mine), axis=1, keepdims=True) * rate
        own_square[at, :] = jnp.broadcast_to(square, (step, 128))
        if also is not None:
            also(at)
        return carry

    lax.fori_loop(0, own_ref.shape[0] // step, rows, 0)


def near_kernel(count, h_ref, own_ref, *refs):
    parts, scores = refs[:count], refs[count : 2 * count]
    out_ref, total, x_buf, d_buf, own_square, col_square, sems = refs[2 * count :]
    rows, knots = own_ref.shape
    scale, rate = 2.0 / h_ref[0], LOG2E / h_ref[0]
    step, tile = 32, 256

    def copies(b):
        return (
            pltpu.make_async_copy(parts[b], x_buf.at[b], sems.at[b, 0]),
            pltpu.make_async_copy(scores[b], d_buf.at[b], sems.at[b, 1]),
        )

    for b in range(count):
        for copy in copies(b):
            copy.start()

    def clear(at):
        out_ref[at, :] = jnp.zeros((step, knots), jnp.float32)
        total[at, :] = jnp.zeros((step, 128), jnp.float32)

    prepare_rows(own_ref, own_square, rate, step, clear)
    for b in range(count):
        for copy in copies(b):
            copy.wait()

    def block(b, carry):
        def columns(t, carry):
            squares = []
            for u in range(0, 128, step):
                at = pl.ds(pl.multiple_of(t * 128 + u, step), step)
                x = x_buf[b, at, :].astype(jnp.float32)
                d = d_buf[b, at, :].astype(jnp.float32) - scale * x
                d_buf[b, at, :] = d.astype(jnp.bfloat16)
                squares.append(fold(x * x))
            square = jnp.sum(jnp.transpose(jnp.concatenate(squares, axis=0)), axis=0, keepdims=True)
            at = pl.ds(pl.multiple_of(t * 128, 128), 128)
            col_square[:, at] = jnp.broadcast_to(square * rate, (8, 128))
            return carry

        lax.fori_loop(0, rows // 128, columns, 0)

        def one(t, carry):
            at = pl.ds(pl.multiple_of(t // (rows // tile) * tile, tile), tile)
            to = pl.ds(pl.multiple_of(t % (rows // tile) * tile, tile), tile)
            products = lax.dot_general(
                own_ref[at, :], x_buf[b, to, :], PRODUCT, preferred_element_type=jnp.float32
            )
            mine = jnp.concatenate([own_square[at, :]] * (tile // 128), axis=1)
            kernel = jnp.exp2(products * (2.0 * rate) - (mine + col_square[:1, to]))
            total[at, :] += fold(kernel)
            out_ref[at, :] += jnp.dot(
                kernel.astype(jnp.bfloat16), d_buf[b, to, :], preferred_element_type=jnp.float32
            )
            return carry

        lax.fori_loop(0, (rows // tile) ** 2, one, 0)
        return carry

    lax.fori_loop(0, count, block, 0)


def far_kernel(count, choice, last, h_ref, flag_ref, own_ref, *refs):
    names = count if choice is None else count + 1
    parts, scores = refs[:names], refs[names : names + count]
    sum_in, total_in, out_ref = refs[names + count : names + count + 3]
    refs = refs[names + count + 3 :]
    if not last:
        total_out = refs[0]
        refs = refs[1:]
    x_buf, s_buf, own_square, total, sems, sum_sems = refs
    rows, knots = own_ref.shape
    scale, rate = 2.0 / h_ref[0], LOG2E / h_ref[0]

    def part_copy(b, source):
        return pltpu.make_async_copy(source, x_buf.at[b], sems.at[b, 0])

    def score_copy(b):
        return pltpu.make_async_copy(scores[b], s_buf.at[b], sems.at[b, 1])

    sums = (
        pltpu.make_async_copy(sum_in, out_ref, sum_sems.at[0]),
        pltpu.make_async_copy(total_in, total, sum_sems.at[1]),
    )
    for b in range(count):
        if b == choice:
            pl.when(flag_ref[0] == 0)(lambda: part_copy(b, parts[b]).start())
            pl.when(flag_ref[0] != 0)(lambda: part_copy(b, parts[count]).start())
        else:
            part_copy(b, parts[b]).start()
        score_copy(b).start()
        if b == 0:
            for copy in sums:
                copy.start()

    prepare_rows(own_ref, own_square, rate, 256)
    for copy in sums:
        copy.wait()

    def block(b, carry):
        part_copy(b, parts[0]).wait()
        pltpu.make_async_copy(scores[0], s_buf.at[b], sems.at[b, 1]).wait()
        x = x_buf[b].astype(jnp.float32)
        drift = (s_buf[b].astype(jnp.float32) - scale * x).astype(jnp.bfloat16)
        square = jnp.sum(jnp.transpose(fold(x * x)), axis=0, keepdims=True) * rate
        products = lax.dot_general(
            own_ref[...], x_buf[b], PRODUCT, preferred_element_type=jnp.float32
        )
        mine = jnp.concatenate([own_square[...]] * (rows // 128), axis=1)
        kernel = jnp.exp2(products * (2.0 * rate) - (mine + square))
        total[...] += fold(kernel)
        out_ref[...] += jnp.dot(
            kernel.astype(jnp.bfloat16), drift, preferred_element_type=jnp.float32
        )
        return carry

    lax.fori_loop(0, count, block, 0)

    def finish(t, carry):
        at = pl.ds(pl.multiple_of(t * 256, 256), 256)
        if last:
            mine = own_ref[at, :].astype(jnp.float32)
            out_ref[at, :] += scale * mine * jnp.sum(total[at, :], axis=1, keepdims=True)
        else:
            total_out[at, :] = total[at, :]
        return carry

    lax.fori_loop(0, rows // 256, finish, 0)


SMEM = pl.BlockSpec(memory_space=pltpu.SMEM)
VMEM = pl.BlockSpec(memory_space=pltpu.VMEM)
ANY = pl.BlockSpec(memory_space=pl.ANY)


def common(count, rows, knots, mebibytes):
    return dict(
        cost_estimate=pl.CostEstimate(
            flops=4 * count * rows * rows * knots,
            bytes_accessed=4 * (count + 2) * rows * knots,
            transcendentals=count * rows * rows,
        ),
        compiler_params=pltpu.CompilerParams(vmem_limit_bytes=mebibytes * 1024 * 1024),
    )


def near_terms(spread, own, blocks):
    rows, knots = own.shape
    count = len(blocks)
    return pl.pallas_call(
        functools.partial(near_kernel, count),
        out_shape=[
            jax.ShapeDtypeStruct((rows, knots), jnp.float32),
            jax.ShapeDtypeStruct((rows, 128), jnp.float32),
        ],
        in_specs=[SMEM, VMEM] + [ANY] * (2 * count),
        out_specs=[VMEM, VMEM],
        scratch_shapes=[
            pltpu.VMEM((count, rows, knots), jnp.bfloat16),
            pltpu.VMEM((count, rows, knots), jnp.bfloat16),
            pltpu.VMEM((rows, 128), jnp.float32),
            pltpu.VMEM((8, rows), jnp.float32),
            pltpu.SemaphoreType.DMA((count, 2)),
        ],
        **common(count, rows, knots, 16),
    )(spread, own, *[b[0] for b in blocks], *[b[1] for b in blocks])


def far_terms(spread, flag, own, blocks, running, last, choice=None, other=None):
    rows, knots = own.shape
    count = len(blocks)
    parts = [b[0] for b in blocks] + ([] if choice is None else [other])
    out_shape = [jax.ShapeDtypeStruct((rows, knots), jnp.float32)]
    if not last:
        out_shape.append(jax.ShapeDtypeStruct((rows, 128), jnp.float32))
    return pl.pallas_call(
        functools.partial(far_kernel, count, choice, last),
        out_shape=out_shape,
        in_specs=[SMEM, SMEM, VMEM] + [ANY] * (len(parts) + count + 2),
        out_specs=[VMEM] * len(out_shape),
        scratch_shapes=[
            pltpu.VMEM((count, rows, knots), jnp.bfloat16),
            pltpu.VMEM((count, rows, knots), jnp.bfloat16),
            pltpu.VMEM((rows, 128), jnp.float32),
            pltpu.VMEM((rows, 128), jnp.float32),
            pltpu.SemaphoreType.DMA((count, 2)),
            pltpu.SemaphoreType.DMA((2,)),
        ],
        **common(count, rows, knots, 14 + 4 * count),
    )(spread, flag, own, *parts, *[b[1] for b in blocks], *running)


GRAY = [0, 1, 3, 2]
CODE_TO_MOVE = [GRAY.index(c >> 2) * 4 + GRAY.index(c & 3) for c in range(PLANE)]


def to_code(move):
    return move ^ (move >> 1 & 5)


def hop(block, move, pb_move=0):
    bits = move * lax.axis_size("pb") + pb_move
    if bits == 0:
        return block
    count = lax.axis_size(("pa", "pb"))
    return lax.ppermute(block, ("pa", "pb"), [(i, i ^ bits) for i in range(count)])


def rank(option, free):
    place, value = 0, 0
    for k in range(4):
        value = value | (option >> k & 1) << place
        place = place + (free >> k & 1)
    return value


def choose(index, branches, *operands):
    if len(branches) == 1:
        return branches[0](*operands)
    half = len(branches) // 2
    return lax.cond(
        index < half,
        lambda *o: choose(index, branches[:half], *o),
        lambda *o: choose(index - half, branches[half:], *o),
        *operands,
    )


def side_by_side(first, first_code, second, second_code):
    branches = []
    for code in range(PLANE):
        moves = [CODE_TO_MOVE[c] for c in range(PLANE) if c & code == 0]

        def branch(a, b, inner, code=code, moves=moves):
            moved = hop(a, CODE_TO_MOVE[code])
            return moved, choose(inner, [functools.partial(hop, move=move) for move in moves], b)

        branches.append(branch)
    inner = rank(second_code, first_code ^ (PLANE - 1))
    return choose(first_code, branches, first, second, inner)


def per_device(particles, scores, spread, plan):
    masks = plan[:, 0]
    low, high = jnp.minimum(masks[0], masks[1]), jnp.maximum(masks[0], masks[1])
    low_y, high_y = low >> 4, high >> 4
    low_code, high_code = to_code(low & 15), to_code(high & 15)
    shared = low_code & high_code

    mate = (hop(particles, 0, 1), hop(scores, 0, 1))
    base = lax.cond(low_y == 1, functools.partial(hop, move=Y_NEXT), lambda x: x, particles)
    base, early_scores = lax.optimization_barrier((base, scores))
    scores_y = hop(early_scores, Y_NEXT)

    def first_slot(move, base, spread, particles, scores, *mate):
        near = near_terms(spread, particles, [(particles, scores), mate])
        return hop(base, move), near

    part_way, running = choose(
        shared,
        [functools.partial(first_slot, CODE_TO_MOVE[c]) for c in range(PLANE)],
        *(base, spread, particles, scores, *mate),
    )

    late_particles, part_way = lax.optimization_barrier((particles, part_way))
    parts_far = hop(late_particles, 0, 2)
    low_scores, high_parts = side_by_side(
        jnp.where(low_y == 1, scores_y, scores), low_code, part_way, high_code & ~shared
    )

    late_scores, part_way, high_parts, parts_far = lax.optimization_barrier(
        (scores_y, part_way, high_parts, parts_far)
    )
    scores_far = hop(late_scores, Y_NEXT, 2)
    high_parts_y = hop(high_parts, Y_NEXT)
    parts_far_mate = hop(parts_far, 0, 1)
    high_scores, low_parts = side_by_side(
        jnp.where(high_y == 1, scores_y, scores), high_code, part_way, low_code & ~shared
    )

    flag = (high_y & ~low_y).reshape(1)
    scores_far, low_parts = lax.optimization_barrier((scores_far, low_parts))
    scores_far_mate = hop(scores_far, 0, 1)
    running = far_terms(
        spread,
        flag,
        particles,
        [(low_parts, low_scores), (high_parts, high_scores), (parts_far, scores_far)],
        running,
        last=False,
        choice=1,
        other=high_parts_y,
    )
    return far_terms(
        spread, flag, particles, [(parts_far_mate, scores_far_mate)], running, last=True
    )[0]


def solution(mesh):
    in_specs = (P(("pa", "pb"), None), P(("pa", "pb"), None), P(), P())
    out_specs = P(("pa", "pb"), None)
    return jax.shard_map(
        per_device, mesh=mesh, in_specs=in_specs, out_specs=out_specs, check_vma=False
    )
```

```python
import functools

import jax
import jax.numpy as jnp
from jax import lax
from jax.experimental import pallas as pl
from jax.experimental.pallas import tpu as pltpu
from jax.sharding import PartitionSpec as P

LOG2E = 1.4426950408889634
Y_NEXT = 16
PLANE = 16
PRODUCT = (((1,), (1,)), ((), ()))


def fold(square):
    total = square[:, :128]
    for i in range(128, square.shape[1], 128):
        total = total + square[:, i : i + 128]
    return total


def terms_kernel(count, first, last, choice, h_ref, flag_ref, own_ref, *refs):
    names = count if choice is None else count + 1
    parts, scores = refs[:names], refs[names : names + count]
    refs = refs[names + count :]
    if not first:
        sum_in, total_in = refs[:2]
        refs = refs[2:]
    out_ref = refs[0]
    refs = refs[1:]
    if not last:
        total_out = refs[0]
        refs = refs[1:]
    x_buf, s_buf, own_square, total, sems, sum_sems = refs
    rows, knots = own_ref.shape
    scale, rate = 2.0 / h_ref[0], LOG2E / h_ref[0]
    step, tile = 256, 384

    def part_copy(b, source):
        return pltpu.make_async_copy(source, x_buf.at[b], sems.at[b, 0])

    def score_copy(b, source):
        return pltpu.make_async_copy(source, s_buf.at[b], sems.at[b, 1])

    if not first:
        sums = (
            pltpu.make_async_copy(sum_in, out_ref, sum_sems.at[0]),
            pltpu.make_async_copy(total_in, total, sum_sems.at[1]),
        )
    for b in range(count):
        if b == choice:
            pl.when(flag_ref[0] == 0)(lambda: part_copy(b, parts[b]).start())
            pl.when(flag_ref[0] != 0)(lambda: part_copy(b, parts[count]).start())
        else:
            part_copy(b, parts[b]).start()
        score_copy(b, scores[b]).start()
        if b == 0 and not first:
            for copy in sums:
                copy.start()

    def prepare(t, carry):
        at = pl.ds(pl.multiple_of(t * step, step), step)
        mine = own_ref[at, :].astype(jnp.float32)
        square = jnp.sum(fold(mine * mine), axis=1, keepdims=True) * rate
        own_square[at, :] = jnp.broadcast_to(square, (step, 128))
        if first:
            out_ref[at, :] = jnp.zeros((step, knots), jnp.float32)
            total[at, :] = jnp.zeros((step, 128), jnp.float32)
        return carry

    lax.fori_loop(0, rows // step, prepare, 0)
    if not first:
        for copy in sums:
            copy.wait()

    def block(b, carry):
        part_copy(b, parts[0]).wait()
        score_copy(b, scores[0]).wait()

        def columns(t, carry):
            at = pl.ds(pl.multiple_of(t * tile, tile), tile)
            x = x_buf[b, at, :].astype(jnp.float32)
            drift = (s_buf[b, at, :].astype(jnp.float32) - scale * x).astype(jnp.bfloat16)
            square = jnp.sum(jnp.transpose(fold(x * x)), axis=0, keepdims=True) * rate
            products = lax.dot_general(
                own_ref[...], x_buf[b, at, :], PRODUCT, preferred_element_type=jnp.float32
            )
            mine = jnp.concatenate([own_square[...]] * (tile // 128), axis=1)
            kernel = jnp.exp2(products * (2.0 * rate) - (mine + square))
            total[...] += fold(kernel)
            out_ref[...] += jnp.dot(
                kernel.astype(jnp.bfloat16), drift, preferred_element_type=jnp.float32
            )
            return carry

        return lax.fori_loop(0, rows // tile, columns, carry)

    lax.fori_loop(0, count, block, 0)

    def finish(t, carry):
        at = pl.ds(pl.multiple_of(t * step, step), step)
        if last:
            mine = own_ref[at, :].astype(jnp.float32)
            out_ref[at, :] += scale * mine * jnp.sum(total[at, :], axis=1, keepdims=True)
        else:
            total_out[at, :] = total[at, :]
        return carry

    lax.fori_loop(0, rows // step, finish, 0)


def add_terms(spread, flag, own, blocks, running=(), last=False, choice=None, other=None):
    rows, knots = own.shape
    count = len(blocks)
    parts = [b[0] for b in blocks] + ([] if choice is None else [other])
    smem, vmem = pl.BlockSpec(memory_space=pltpu.SMEM), pl.BlockSpec(memory_space=pltpu.VMEM)
    anywhere = pl.BlockSpec(memory_space=pl.ANY)
    out_shape = [jax.ShapeDtypeStruct((rows, knots), jnp.float32)]
    if not last:
        out_shape.append(jax.ShapeDtypeStruct((rows, 128), jnp.float32))
    return pl.pallas_call(
        functools.partial(terms_kernel, count, not running, last, choice),
        out_shape=out_shape,
        in_specs=[smem, smem, vmem] + [anywhere] * (len(parts) + count + len(running)),
        out_specs=[vmem] * len(out_shape),
        scratch_shapes=[
            pltpu.VMEM((count, rows, knots), jnp.bfloat16),
            pltpu.VMEM((count, rows, knots), jnp.bfloat16),
            pltpu.VMEM((rows, 128), jnp.float32),
            pltpu.VMEM((rows, 128), jnp.float32),
            pltpu.SemaphoreType.DMA((count, 2)),
            pltpu.SemaphoreType.DMA((2,)),
        ],
        cost_estimate=pl.CostEstimate(
            flops=4 * count * rows * rows * knots,
            bytes_accessed=4 * (count + 2) * rows * knots,
            transcendentals=count * rows * rows,
        ),
        compiler_params=pltpu.CompilerParams(vmem_limit_bytes=(14 + 4 * count) * 1024 * 1024),
    )(spread, flag, own, *parts, *[b[1] for b in blocks], *running)


GRAY = [0, 1, 3, 2]
CODE_TO_MOVE = [GRAY.index(c >> 2) * 4 + GRAY.index(c & 3) for c in range(PLANE)]


def to_code(move):
    return move ^ (move >> 1 & 5)


def hop(block, move, pb_move=0):
    bits = move * lax.axis_size("pb") + pb_move
    if bits == 0:
        return block
    count = lax.axis_size(("pa", "pb"))
    return lax.ppermute(block, ("pa", "pb"), [(i, i ^ bits) for i in range(count)])


def rank(option, free):
    place, value = 0, 0
    for k in range(4):
        value = value | (option >> k & 1) << place
        place = place + (free >> k & 1)
    return value


def side_by_side(first, first_code, second, second_code):
    branches = []
    for code in range(PLANE):
        moves = [CODE_TO_MOVE[c] for c in range(PLANE) if c & code == 0]

        def branch(a, b, inner, code=code, moves=moves):
            moved = hop(a, CODE_TO_MOVE[code])
            return moved, lax.switch(
                inner, [functools.partial(hop, move=move) for move in moves], b
            )

        branches.append(branch)
    inner = rank(second_code, first_code ^ (PLANE - 1))
    return lax.switch(first_code, branches, first, second, inner)


def per_device(particles, scores, spread, plan):
    masks = plan[:, 0]
    low, high = jnp.minimum(masks[0], masks[1]), jnp.maximum(masks[0], masks[1])
    low_y, high_y = low >> 4, high >> 4
    low_code, high_code = to_code(low & 15), to_code(high & 15)
    shared = low_code & high_code

    flag = (high_y & ~low_y).reshape(1)
    both_y = low_y & high_y

    scores_y = hop(scores, Y_NEXT)
    mate = (hop(particles, 0, 1), hop(scores, 0, 1))

    moves = [CODE_TO_MOVE[c] + y for y in (0, Y_NEXT) for c in range(PLANE)]
    part_way = lax.switch(
        shared | both_y << 4, [functools.partial(hop, move=move) for move in moves], particles
    )

    late_particles, part_way = lax.optimization_barrier((particles, part_way))
    parts_far = hop(late_particles, 0, 2)
    running = add_terms(spread, flag, late_particles, [(late_particles, scores)])
    low_start = jnp.where(low_y == 1, scores_y, scores)
    low_start, part_way, running = lax.optimization_barrier((low_start, part_way, running))
    low_scores, high_parts = side_by_side(low_start, low_code, part_way, high_code & ~shared)

    late_scores, part_way, high_parts, parts_far, running, mate = lax.optimization_barrier(
        (scores_y, part_way, high_parts, parts_far, running, mate)
    )
    scores_far = hop(late_scores, Y_NEXT, 2)
    high_parts_y = hop(high_parts, Y_NEXT)
    parts_far_mate = hop(parts_far, 0, 1)
    running = add_terms(spread, flag, particles, [mate], running)
    high_start = jnp.where(high_y == 1, scores_y, scores)
    high_start, part_way, running = lax.optimization_barrier((high_start, part_way, running))
    high_scores, low_parts = side_by_side(high_start, high_code, part_way, low_code & ~shared)

    scores_far, low_parts = lax.optimization_barrier((scores_far, low_parts))
    scores_far_mate = hop(scores_far, 0, 1)
    running = add_terms(
        spread,
        flag,
        particles,
        [(low_parts, low_scores), (high_parts, high_scores), (parts_far, scores_far)],
        running,
        choice=1,
        other=high_parts_y,
    )
    return add_terms(
        spread, flag, particles, [(parts_far_mate, scores_far_mate)], running, last=True
    )[0]


def solution(mesh):
    in_specs = (P(("pa", "pb"), None), P(("pa", "pb"), None), P(), P())
    out_specs = P(("pa", "pb"), None)
    return jax.shard_map(
        per_device, mesh=mesh, in_specs=in_specs, out_specs=out_specs, check_vma=False
    )
```

```python
import functools

import jax
import jax.numpy as jnp
from jax import lax
from jax.experimental import pallas as pl
from jax.experimental.pallas import tpu as pltpu
from jax.sharding import PartitionSpec as P

LOG2E = 1.4426950408889634
Y_NEXT = 16
PLANE = 16
PRODUCT = (((1,), (1,)), ((), ()))


def fold(square):
    total = square[:, :128]
    for i in range(128, square.shape[1], 128):
        total = total + square[:, i : i + 128]
    return total


def prepare_rows(own_ref, own_square, rate, step, also=None):
    def rows(t, carry):
        at = pl.ds(pl.multiple_of(t * step, step), step)
        mine = own_ref[at, :].astype(jnp.float32)
        square = jnp.sum(fold(mine * mine), axis=1, keepdims=True) * rate
        own_square[at, :] = jnp.broadcast_to(square, (step, 128))
        if also is not None:
            also(at)
        return carry

    lax.fori_loop(0, own_ref.shape[0] // step, rows, 0)


def near_kernel(count, h_ref, own_ref, *refs):
    parts, scores = refs[:count], refs[count : 2 * count]
    out_ref, total, x_buf, d_buf, own_square, col_square, sems = refs[2 * count :]
    rows, knots = own_ref.shape
    scale, rate = 2.0 / h_ref[0], LOG2E / h_ref[0]
    step, tile = 32, 256

    def copies(b):
        return (
            pltpu.make_async_copy(parts[b], x_buf.at[b], sems.at[b, 0]),
            pltpu.make_async_copy(scores[b], d_buf.at[b], sems.at[b, 1]),
        )

    for b in range(count):
        for copy in copies(b):
            copy.start()

    def clear(at):
        out_ref[at, :] = jnp.zeros((step, knots), jnp.float32)
        total[at, :] = jnp.zeros((step, 128), jnp.float32)

    prepare_rows(own_ref, own_square, rate, step, clear)
    for b in range(count):
        for copy in copies(b):
            copy.wait()

    def block(b, carry):
        def columns(t, carry):
            squares = []
            for u in range(0, 128, step):
                at = pl.ds(pl.multiple_of(t * 128 + u, step), step)
                x = x_buf[b, at, :].astype(jnp.float32)
                d = d_buf[b, at, :].astype(jnp.float32) - scale * x
                d_buf[b, at, :] = d.astype(jnp.bfloat16)
                squares.append(fold(x * x))
            square = jnp.sum(jnp.transpose(jnp.concatenate(squares, axis=0)), axis=0, keepdims=True)
            at = pl.ds(pl.multiple_of(t * 128, 128), 128)
            col_square[:, at] = jnp.broadcast_to(square * rate, (8, 128))
            return carry

        lax.fori_loop(0, rows // 128, columns, 0)

        def one(t, carry):
            at = pl.ds(pl.multiple_of(t // (rows // tile) * tile, tile), tile)
            to = pl.ds(pl.multiple_of(t % (rows // tile) * tile, tile), tile)
            products = lax.dot_general(
                own_ref[at, :], x_buf[b, to, :], PRODUCT, preferred_element_type=jnp.float32
            )
            mine = jnp.concatenate([own_square[at, :]] * (tile // 128), axis=1)
            kernel = jnp.exp2(products * (2.0 * rate) - (mine + col_square[:1, to]))
            total[at, :] += fold(kernel)
            out_ref[at, :] += jnp.dot(
                kernel.astype(jnp.bfloat16), d_buf[b, to, :], preferred_element_type=jnp.float32
            )
            return carry

        lax.fori_loop(0, (rows // tile) ** 2, one, 0)
        return carry

    lax.fori_loop(0, count, block, 0)


def far_kernel(count, choice, last, h_ref, flag_ref, own_ref, *refs):
    names = count if choice is None else count + 1
    parts, scores = refs[:names], refs[names : names + count]
    sum_in, total_in, out_ref = refs[names + count : names + count + 3]
    refs = refs[names + count + 3 :]
    if not last:
        total_out = refs[0]
        refs = refs[1:]
    x_buf, s_buf, own_square, total, sems, sum_sems = refs
    rows, knots = own_ref.shape
    scale, rate = 2.0 / h_ref[0], LOG2E / h_ref[0]

    def part_copy(b, source):
        return pltpu.make_async_copy(source, x_buf.at[b], sems.at[b, 0])

    def score_copy(b):
        return pltpu.make_async_copy(scores[b], s_buf.at[b], sems.at[b, 1])

    sums = (
        pltpu.make_async_copy(sum_in, out_ref, sum_sems.at[0]),
        pltpu.make_async_copy(total_in, total, sum_sems.at[1]),
    )
    for b in range(count):
        if b == choice:
            pl.when(flag_ref[0] == 0)(lambda: part_copy(b, parts[b]).start())
            pl.when(flag_ref[0] != 0)(lambda: part_copy(b, parts[count]).start())
        else:
            part_copy(b, parts[b]).start()
        score_copy(b).start()
        if b == 0:
            for copy in sums:
                copy.start()

    prepare_rows(own_ref, own_square, rate, 256)
    for copy in sums:
        copy.wait()

    def block(b, carry):
        part_copy(b, parts[0]).wait()
        pltpu.make_async_copy(scores[0], s_buf.at[b], sems.at[b, 1]).wait()
        x = x_buf[b].astype(jnp.float32)
        drift = (s_buf[b].astype(jnp.float32) - scale * x).astype(jnp.bfloat16)
        square = jnp.sum(jnp.transpose(fold(x * x)), axis=0, keepdims=True) * rate
        products = lax.dot_general(
            own_ref[...], x_buf[b], PRODUCT, preferred_element_type=jnp.float32
        )
        mine = jnp.concatenate([own_square[...]] * (rows // 128), axis=1)
        kernel = jnp.exp2(products * (2.0 * rate) - (mine + square))
        total[...] += fold(kernel)
        out_ref[...] += jnp.dot(
            kernel.astype(jnp.bfloat16), drift, preferred_element_type=jnp.float32
        )
        return carry

    lax.fori_loop(0, count, block, 0)

    def finish(t, carry):
        at = pl.ds(pl.multiple_of(t * 256, 256), 256)
        if last:
            mine = own_ref[at, :].astype(jnp.float32)
            out_ref[at, :] += scale * mine * jnp.sum(total[at, :], axis=1, keepdims=True)
        else:
            total_out[at, :] = total[at, :]
        return carry

    lax.fori_loop(0, rows // 256, finish, 0)


SMEM = pl.BlockSpec(memory_space=pltpu.SMEM)
VMEM = pl.BlockSpec(memory_space=pltpu.VMEM)
ANY = pl.BlockSpec(memory_space=pl.ANY)


def common(count, rows, knots, mebibytes):
    return dict(
        cost_estimate=pl.CostEstimate(
            flops=4 * count * rows * rows * knots,
            bytes_accessed=4 * (count + 2) * rows * knots,
            transcendentals=count * rows * rows,
        ),
        compiler_params=pltpu.CompilerParams(vmem_limit_bytes=mebibytes * 1024 * 1024),
    )


def near_terms(spread, own, blocks):
    rows, knots = own.shape
    count = len(blocks)
    return pl.pallas_call(
        functools.partial(near_kernel, count),
        out_shape=[
            jax.ShapeDtypeStruct((rows, knots), jnp.float32),
            jax.ShapeDtypeStruct((rows, 128), jnp.float32),
        ],
        in_specs=[SMEM, VMEM] + [ANY] * (2 * count),
        out_specs=[VMEM, VMEM],
        scratch_shapes=[
            pltpu.VMEM((count, rows, knots), jnp.bfloat16),
            pltpu.VMEM((count, rows, knots), jnp.bfloat16),
            pltpu.VMEM((rows, 128), jnp.float32),
            pltpu.VMEM((8, rows), jnp.float32),
            pltpu.SemaphoreType.DMA((count, 2)),
        ],
        **common(count, rows, knots, 12),
    )(spread, own, *[b[0] for b in blocks], *[b[1] for b in blocks])


def far_terms(spread, flag, own, blocks, running, last, choice=None, other=None):
    rows, knots = own.shape
    count = len(blocks)
    parts = [b[0] for b in blocks] + ([] if choice is None else [other])
    out_shape = [jax.ShapeDtypeStruct((rows, knots), jnp.float32)]
    if not last:
        out_shape.append(jax.ShapeDtypeStruct((rows, 128), jnp.float32))
    return pl.pallas_call(
        functools.partial(far_kernel, count, choice, last),
        out_shape=out_shape,
        in_specs=[SMEM, SMEM, VMEM] + [ANY] * (len(parts) + count + 2),
        out_specs=[VMEM] * len(out_shape),
        scratch_shapes=[
            pltpu.VMEM((count, rows, knots), jnp.bfloat16),
            pltpu.VMEM((count, rows, knots), jnp.bfloat16),
            pltpu.VMEM((rows, 128), jnp.float32),
            pltpu.VMEM((rows, 128), jnp.float32),
            pltpu.SemaphoreType.DMA((count, 2)),
            pltpu.SemaphoreType.DMA((2,)),
        ],
        **common(count, rows, knots, 11 + 4 * count),
    )(spread, flag, own, *parts, *[b[1] for b in blocks], *running)


GRAY = [0, 1, 3, 2]
CODE_TO_MOVE = [GRAY.index(c >> 2) * 4 + GRAY.index(c & 3) for c in range(PLANE)]


def to_code(move):
    return move ^ (move >> 1 & 5)


def hop(block, move, pb_move=0):
    bits = move * lax.axis_size("pb") + pb_move
    if bits == 0:
        return block
    count = lax.axis_size(("pa", "pb"))
    return lax.ppermute(block, ("pa", "pb"), [(i, i ^ bits) for i in range(count)])


def rank(option, free):
    place, value = 0, 0
    for k in range(4):
        value = value | (option >> k & 1) << place
        place = place + (free >> k & 1)
    return value


def side_by_side(first, first_code, second, second_code, stay=None):
    branches = []
    for code in range(PLANE):
        moves = [CODE_TO_MOVE[c] for c in range(PLANE) if code and c & code == 0]

        def branch(a, b, kept, inner, code=code, moves=moves):
            def fresh(x, y):
                return jnp.where(inner >= 0, x, y)

            def moved(b, kept, move=0):
                return hop(b, move) if move else fresh(b, a)

            choices = [functools.partial(moved, move=move) for move in moves or [0]]
            if stay is not None:
                choices.append(lambda b, kept: fresh(kept, a))
            result = hop(a, CODE_TO_MOVE[code]) if code else fresh(a, b)
            return result, lax.switch(inner, choices, b, kept)

        branches.append(branch)
    free = first_code ^ (PLANE - 1)
    inner = jnp.where(second_code < 0, 16, rank(second_code, free))
    return lax.switch(
        first_code, branches, first, second, second if stay is None else stay, inner
    )


def per_device(particles, scores, spread, plan):
    masks = plan[:, 0]
    swap = (masks[0] ^ 15) > (masks[1] ^ 15)
    low, high = jnp.where(swap, masks[1], masks[0]), jnp.where(swap, masks[0], masks[1])
    low_y, high_y = low >> 4, high >> 4
    low_code, high_code = to_code(low & 15), to_code(high & 15)
    straight = high_code == 0
    shared = jnp.where(straight, low_code, low_code & high_code)

    mate = (hop(particles, 0, 1), hop(scores, 0, 1))
    base = lax.cond(low_y == 1, functools.partial(hop, move=Y_NEXT), lambda x: x, particles)
    base, early_scores = lax.optimization_barrier((base, scores))
    scores_y = hop(early_scores, Y_NEXT)

    def first_slot(move, base, spread, particles, scores, *mate):
        near = near_terms(spread, particles, [(particles, scores), mate])
        return hop(base, move), near

    part_way, running = lax.switch(
        shared,
        [functools.partial(first_slot, CODE_TO_MOVE[c]) for c in range(PLANE)],
        *(base, spread, particles, scores, *mate),
    )

    late_particles, part_way = lax.optimization_barrier((particles, part_way))
    parts_far = hop(late_particles, 0, 2)
    low_scores, high_parts = side_by_side(
        jnp.where(low_y == 1, scores_y, scores),
        low_code,
        part_way,
        jnp.where(straight, -1, high_code & ~shared),
        base,
    )

    late_scores, part_way, high_parts, parts_far = lax.optimization_barrier(
        (scores_y, part_way, high_parts, parts_far)
    )
    scores_far = hop(late_scores, Y_NEXT, 2)
    high_parts_y = hop(high_parts, Y_NEXT)
    parts_far_mate = hop(parts_far, 0, 1)
    high_scores, low_parts = side_by_side(
        jnp.where(high_y == 1, scores_y, scores), high_code, part_way, low_code & ~shared
    )

    flag = (high_y & ~low_y).reshape(1)
    scores_far, low_parts = lax.optimization_barrier((scores_far, low_parts))
    scores_far_mate = hop(scores_far, 0, 1)
    running = far_terms(
        spread,
        flag,
        particles,
        [(low_parts, low_scores), (high_parts, high_scores), (parts_far, scores_far)],
        running,
        last=False,
        choice=1,
        other=high_parts_y,
    )
    return far_terms(
        spread, flag, particles, [(parts_far_mate, scores_far_mate)], running, last=True
    )[0]


def solution(mesh):
    in_specs = (P(("pa", "pb"), None), P(("pa", "pb"), None), P(), P())
    out_specs = P(("pa", "pb"), None)
    return jax.shard_map(
        per_device, mesh=mesh, in_specs=in_specs, out_specs=out_specs, check_vma=False
    )
```

```python
import functools

import jax
import jax.numpy as jnp
from jax import lax
from jax.experimental import pallas as pl
from jax.experimental.pallas import tpu as pltpu
from jax.sharding import PartitionSpec as P

LOG2E = 1.4426950408889634
Y_NEXT = 16
PLANE = 16
PRODUCT = (((1,), (1,)), ((), ()))


def fold(square):
    total = square[:, :128]
    for i in range(128, square.shape[1], 128):
        total = total + square[:, i : i + 128]
    return total


def prepare_rows(own_ref, own_square, rate, step, also=None):
    def rows(t, carry):
        at = pl.ds(pl.multiple_of(t * step, step), step)
        mine = own_ref[at, :].astype(jnp.float32)
        square = jnp.sum(fold(mine * mine), axis=1, keepdims=True) * rate
        own_square[at, :] = jnp.broadcast_to(square, (step, 128))
        if also is not None:
            also(at)
        return carry

    lax.fori_loop(0, own_ref.shape[0] // step, rows, 0)


def near_kernel(count, h_ref, own_in, *refs):
    parts, scores = refs[:count], refs[count : 2 * count]
    out_ref, total, own_ref, x_buf, d_buf, own_square, col_square, sems, own_sem = refs[2 * count :]
    rows, knots = own_ref.shape
    own_copy = pltpu.make_async_copy(own_in, own_ref, own_sem)
    own_copy.start()
    scale, rate = 2.0 / h_ref[0], LOG2E / h_ref[0]
    step, tile = 32, 256

    def copies(b):
        return (
            pltpu.make_async_copy(parts[b], x_buf.at[b], sems.at[b, 0]),
            pltpu.make_async_copy(scores[b], d_buf.at[b], sems.at[b, 1]),
        )

    for b in range(count):
        for copy in copies(b):
            copy.start()

    def clear(at):
        out_ref[at, :] = jnp.zeros((step, knots), jnp.float32)
        total[at, :] = jnp.zeros((step, 128), jnp.float32)

    own_copy.wait()
    prepare_rows(own_ref, own_square, rate, step, clear)
    for b in range(count):
        for copy in copies(b):
            copy.wait()

    def block(b, carry):
        def columns(t, carry):
            squares = []
            for u in range(0, 128, step):
                at = pl.ds(pl.multiple_of(t * 128 + u, step), step)
                x = x_buf[b, at, :].astype(jnp.float32)
                d = d_buf[b, at, :].astype(jnp.float32) - scale * x
                d_buf[b, at, :] = d.astype(jnp.bfloat16)
                squares.append(fold(x * x))
            square = jnp.sum(jnp.transpose(jnp.concatenate(squares, axis=0)), axis=0, keepdims=True)
            at = pl.ds(pl.multiple_of(t * 128, 128), 128)
            col_square[:, at] = jnp.broadcast_to(square * rate, (8, 128))
            return carry

        lax.fori_loop(0, rows // 128, columns, 0)

        def one(t, carry):
            at = pl.ds(pl.multiple_of(t // (rows // tile) * tile, tile), tile)
            to = pl.ds(pl.multiple_of(t % (rows // tile) * tile, tile), tile)
            products = lax.dot_general(
                own_ref[at, :], x_buf[b, to, :], PRODUCT, preferred_element_type=jnp.float32
            )
            mine = jnp.concatenate([own_square[at, :]] * (tile // 128), axis=1)
            kernel = jnp.exp2(products * (2.0 * rate) - (mine + col_square[:1, to]))
            total[at, :] += fold(kernel)
            out_ref[at, :] += jnp.dot(
                kernel.astype(jnp.bfloat16), d_buf[b, to, :], preferred_element_type=jnp.float32
            )
            return carry

        lax.fori_loop(0, (rows // tile) ** 2, one, 0)
        return carry

    lax.fori_loop(0, count, block, 0)


def far_kernel(count, choice, last, h_ref, flag_ref, own_in, *refs):
    names = count if choice is None else count + 1
    parts, scores = refs[:names], refs[names : names + count]
    sum_in, total_in, out_ref = refs[names + count : names + count + 3]
    refs = refs[names + count + 3 :]
    if not last:
        total_out = refs[0]
        refs = refs[1:]
    own_ref, x_buf, s_buf, own_square, total, sems, sum_sems = refs
    rows, knots = own_ref.shape
    own_copy = pltpu.make_async_copy(own_in, own_ref, sum_sems.at[2])
    own_copy.start()
    scale, rate = 2.0 / h_ref[0], LOG2E / h_ref[0]

    def part_copy(b, source):
        return pltpu.make_async_copy(source, x_buf.at[b], sems.at[b, 0])

    def score_copy(b):
        return pltpu.make_async_copy(scores[b], s_buf.at[b], sems.at[b, 1])

    sums = (
        pltpu.make_async_copy(sum_in, out_ref, sum_sems.at[0]),
        pltpu.make_async_copy(total_in, total, sum_sems.at[1]),
    )
    for b in range(count):
        if b == choice:
            pl.when(flag_ref[0] == 0)(lambda: part_copy(b, parts[b]).start())
            pl.when(flag_ref[0] != 0)(lambda: part_copy(b, parts[count]).start())
        else:
            part_copy(b, parts[b]).start()
        score_copy(b).start()
        if b == 0:
            for copy in sums:
                copy.start()

    own_copy.wait()
    prepare_rows(own_ref, own_square, rate, 256)
    for copy in sums:
        copy.wait()

    def block(b, carry):
        part_copy(b, parts[0]).wait()
        pltpu.make_async_copy(scores[0], s_buf.at[b], sems.at[b, 1]).wait()
        x = x_buf[b].astype(jnp.float32)
        drift = (s_buf[b].astype(jnp.float32) - scale * x).astype(jnp.bfloat16)
        square = jnp.sum(jnp.transpose(fold(x * x)), axis=0, keepdims=True) * rate
        products = lax.dot_general(
            own_ref[...], x_buf[b], PRODUCT, preferred_element_type=jnp.float32
        )
        mine = jnp.concatenate([own_square[...]] * (rows // 128), axis=1)
        kernel = jnp.exp2(products * (2.0 * rate) - (mine + square))
        total[...] += fold(kernel)
        out_ref[...] += jnp.dot(
            kernel.astype(jnp.bfloat16), drift, preferred_element_type=jnp.float32
        )
        return carry

    lax.fori_loop(0, count, block, 0)

    def finish(t, carry):
        at = pl.ds(pl.multiple_of(t * 256, 256), 256)
        if last:
            mine = own_ref[at, :].astype(jnp.float32)
            out_ref[at, :] += scale * mine * jnp.sum(total[at, :], axis=1, keepdims=True)
        else:
            total_out[at, :] = total[at, :]
        return carry

    lax.fori_loop(0, rows // 256, finish, 0)


SMEM = pl.BlockSpec(memory_space=pltpu.SMEM)
VMEM = pl.BlockSpec(memory_space=pltpu.VMEM)
ANY = pl.BlockSpec(memory_space=pl.ANY)


def common(count, rows, knots, mebibytes):
    return dict(
        cost_estimate=pl.CostEstimate(
            flops=4 * count * rows * rows * knots,
            bytes_accessed=4 * (count + 2) * rows * knots,
            transcendentals=count * rows * rows,
        ),
        compiler_params=pltpu.CompilerParams(vmem_limit_bytes=mebibytes * 1024 * 1024),
    )


def near_terms(spread, own, blocks):
    rows, knots = own.shape
    count = len(blocks)
    return pl.pallas_call(
        functools.partial(near_kernel, count),
        out_shape=[
            jax.ShapeDtypeStruct((rows, knots), jnp.float32),
            jax.ShapeDtypeStruct((rows, 128), jnp.float32),
        ],
        in_specs=[SMEM] + [ANY] * (1 + 2 * count),
        out_specs=[VMEM, VMEM],
        scratch_shapes=[
            pltpu.VMEM((rows, knots), jnp.bfloat16),
            pltpu.VMEM((count, rows, knots), jnp.bfloat16),
            pltpu.VMEM((count, rows, knots), jnp.bfloat16),
            pltpu.VMEM((rows, 128), jnp.float32),
            pltpu.VMEM((8, rows), jnp.float32),
            pltpu.SemaphoreType.DMA((count, 2)),
            pltpu.SemaphoreType.DMA,
        ],
        **common(count, rows, knots, 14),
    )(spread, own, *[b[0] for b in blocks], *[b[1] for b in blocks])


def far_terms(spread, flag, own, blocks, running, last, choice=None, other=None):
    rows, knots = own.shape
    count = len(blocks)
    parts = [b[0] for b in blocks] + ([] if choice is None else [other])
    out_shape = [jax.ShapeDtypeStruct((rows, knots), jnp.float32)]
    if not last:
        out_shape.append(jax.ShapeDtypeStruct((rows, 128), jnp.float32))
    return pl.pallas_call(
        functools.partial(far_kernel, count, choice, last),
        out_shape=out_shape,
        in_specs=[SMEM, SMEM] + [ANY] * (len(parts) + count + 3),
        out_specs=[VMEM] * len(out_shape),
        scratch_shapes=[
            pltpu.VMEM((rows, knots), jnp.bfloat16),
            pltpu.VMEM((count, rows, knots), jnp.bfloat16),
            pltpu.VMEM((count, rows, knots), jnp.bfloat16),
            pltpu.VMEM((rows, 128), jnp.float32),
            pltpu.VMEM((rows, 128), jnp.float32),
            pltpu.SemaphoreType.DMA((count, 2)),
            pltpu.SemaphoreType.DMA((3,)),
        ],
        **common(count, rows, knots, 13 + 4 * count),
    )(spread, flag, own, *parts, *[b[1] for b in blocks], *running)


GRAY = [0, 1, 3, 2]
CODE_TO_MOVE = [GRAY.index(c >> 2) * 4 + GRAY.index(c & 3) for c in range(PLANE)]


def to_code(move):
    return move ^ (move >> 1 & 5)


def hop(block, move, pb_move=0):
    bits = move * lax.axis_size("pb") + pb_move
    if bits == 0:
        return block
    count = lax.axis_size(("pa", "pb"))
    return lax.ppermute(block, ("pa", "pb"), [(i, i ^ bits) for i in range(count)])


def rank(option, free):
    place, value = 0, 0
    for k in range(4):
        value = value | (option >> k & 1) << place
        place = place + (free >> k & 1)
    return value


def side_by_side(first, first_code, second, inner, stay=None):
    branches = []
    for code in range(PLANE):
        moves = [CODE_TO_MOVE[c] for c in range(PLANE) if code and c & code == 0]

        def branch(a, b, kept, inner, code=code, moves=moves):
            def fresh(x, y):
                return jnp.where(inner >= 0, x, y)

            def moved(b, kept, move=0):
                return hop(b, move) if move else fresh(b, a)

            choices = [functools.partial(moved, move=move) for move in moves or [0]]
            if stay is not None:
                choices.append(lambda b, kept: fresh(kept, a))
            result = hop(a, CODE_TO_MOVE[code]) if code else fresh(a, b)
            return result, lax.switch(inner, choices, b, kept)

        branches.append(branch)
    return lax.switch(
        first_code, branches, first, second, second if stay is None else stay, inner
    )


def route_kernel(plan_ref, *outs):
    one, two = plan_ref[0, 0], plan_ref[1, 0]
    swap = (one ^ 15) > (two ^ 15)
    low, high = jnp.where(swap, two, one), jnp.where(swap, one, two)
    low_y, high_y = low >> 4, high >> 4
    low_code, high_code = to_code(low & 15), to_code(high & 15)
    straight = (high_code == 0).astype(jnp.int32)
    shared = jnp.where(high_code == 0, low_code, low_code & high_code)
    beside_low = rank(high_code & ~shared, low_code ^ (PLANE - 1)) | straight << 4
    beside_high = rank(low_code & ~shared, high_code ^ (PLANE - 1))
    flag = high_y & (1 - low_y | straight)
    values = (shared, low_code, beside_low, high_code, beside_high, low_y, high_y, flag)
    for out, value in zip(outs, values, strict=True):
        out[0] = value


def route(plan):
    smem = pl.BlockSpec(memory_space=pltpu.SMEM)
    return pl.pallas_call(
        route_kernel,
        out_shape=[jax.ShapeDtypeStruct((1,), jnp.int32)] * 8,
        in_specs=[smem],
        out_specs=[smem] * 8,
    )(plan)


def per_device(particles, scores, spread, plan):
    scores_y = hop(scores, Y_NEXT)
    mate = (hop(particles, 0, 1), hop(scores, 0, 1))
    *route_codes, flag = route(plan)
    shared, low_code, beside_low, high_code, beside_high, low_y, high_y = (
        value[0] for value in route_codes
    )

    def first_slot(move, spread, particles, scores, *mate):
        near = near_terms(spread, particles, [(particles, scores), mate])
        return hop(particles, move), near

    part_way, running = lax.switch(
        shared,
        [functools.partial(first_slot, CODE_TO_MOVE[c]) for c in range(PLANE)],
        *(spread, particles, scores, *mate),
    )
    part_way = lax.cond(low_y == 1, functools.partial(hop, move=Y_NEXT), lambda x: x, part_way)

    late_particles, part_way = lax.optimization_barrier((particles, part_way))
    parts_far = hop(late_particles, 0, 2)
    low_scores, high_parts = side_by_side(
        jnp.where(low_y == 1, scores_y, scores), low_code, part_way, beside_low, particles
    )

    late_scores, part_way, high_parts, parts_far = lax.optimization_barrier(
        (scores_y, part_way, high_parts, parts_far)
    )
    scores_far = hop(late_scores, Y_NEXT, 2)
    high_parts_y = hop(high_parts, Y_NEXT)
    parts_far_mate = hop(parts_far, 0, 1)
    high_scores, low_parts = side_by_side(
        jnp.where(high_y == 1, scores_y, scores), high_code, part_way, beside_high
    )

    scores_far, low_parts = lax.optimization_barrier((scores_far, low_parts))
    scores_far_mate = hop(scores_far, 0, 1)
    running = far_terms(
        spread,
        flag,
        particles,
        [(low_parts, low_scores), (high_parts, high_scores), (parts_far, scores_far)],
        running,
        last=False,
        choice=1,
        other=high_parts_y,
    )
    return far_terms(
        spread, flag, particles, [(parts_far_mate, scores_far_mate)], running, last=True
    )[0]


def solution(mesh):
    in_specs = (P(("pa", "pb"), None), P(("pa", "pb"), None), P(), P())
    out_specs = P(("pa", "pb"), None)
    return jax.shard_map(
        per_device, mesh=mesh, in_specs=in_specs, out_specs=out_specs, check_vma=False
    )
```

```python
import functools

import jax
import jax.numpy as jnp
from jax import lax
from jax.experimental import pallas as pl
from jax.experimental.pallas import tpu as pltpu
from jax.sharding import PartitionSpec as P

LOG2E = 1.4426950408889634
Y_NEXT = 16
PLANE = 16
PRODUCT = (((1,), (1,)), ((), ()))


def fold(square):
    total = square[:, :128]
    for i in range(128, square.shape[1], 128):
        total = total + square[:, i : i + 128]
    return total


def prepare_rows(own_ref, own_square, rate, step, also=None):
    def rows(t, carry):
        at = pl.ds(pl.multiple_of(t * step, step), step)
        mine = own_ref[at, :].astype(jnp.float32)
        square = jnp.sum(fold(mine * mine), axis=1, keepdims=True) * rate
        own_square[at, :] = jnp.broadcast_to(square, (step, 128))
        if also is not None:
            also(at)
        return carry

    lax.fori_loop(0, own_ref.shape[0] // step, rows, 0)


def near_kernel(count, h_ref, own_in, *refs):
    parts, scores = [b.at[0] for b in refs[:count]], [b.at[1] for b in refs[:count]]
    out_ref, total, own_ref, x_buf, d_buf, own_square, col_square, sems, own_sem = refs[count:]
    rows, knots = own_ref.shape
    own_copy = pltpu.make_async_copy(own_in.at[0], own_ref, own_sem)
    own_copy.start()
    scale, rate = 2.0 / h_ref[0], LOG2E / h_ref[0]
    step, tile = 32, 256

    def copies(b):
        return (
            pltpu.make_async_copy(parts[b], x_buf.at[b], sems.at[b, 0]),
            pltpu.make_async_copy(scores[b], d_buf.at[b], sems.at[b, 1]),
        )

    for b in range(count):
        for copy in copies(b):
            copy.start()

    def clear(at):
        out_ref[at, :] = jnp.zeros((step, knots), jnp.float32)
        total[at, :] = jnp.zeros((step, 128), jnp.float32)

    own_copy.wait()
    prepare_rows(own_ref, own_square, rate, step, clear)
    for b in range(count):
        for copy in copies(b):
            copy.wait()

    def block(b, carry):
        def columns(t, carry):
            squares = []
            for u in range(0, 128, step):
                at = pl.ds(pl.multiple_of(t * 128 + u, step), step)
                x = x_buf[b, at, :].astype(jnp.float32)
                d = d_buf[b, at, :].astype(jnp.float32) - scale * x
                d_buf[b, at, :] = d.astype(jnp.bfloat16)
                squares.append(fold(x * x))
            square = jnp.sum(jnp.transpose(jnp.concatenate(squares, axis=0)), axis=0, keepdims=True)
            at = pl.ds(pl.multiple_of(t * 128, 128), 128)
            col_square[:, at] = jnp.broadcast_to(square * rate, (8, 128))
            return carry

        lax.fori_loop(0, rows // 128, columns, 0)

        def one(t, carry):
            at = pl.ds(pl.multiple_of(t // (rows // tile) * tile, tile), tile)
            to = pl.ds(pl.multiple_of(t % (rows // tile) * tile, tile), tile)
            products = lax.dot_general(
                own_ref[at, :], x_buf[b, to, :], PRODUCT, preferred_element_type=jnp.float32
            )
            mine = jnp.concatenate([own_square[at, :]] * (tile // 128), axis=1)
            kernel = jnp.exp2(products * (2.0 * rate) - (mine + col_square[:1, to]))
            total[at, :] += fold(kernel)
            out_ref[at, :] += jnp.dot(
                kernel.astype(jnp.bfloat16), d_buf[b, to, :], preferred_element_type=jnp.float32
            )
            return carry

        lax.fori_loop(0, (rows // tile) ** 2, one, 0)
        return carry

    lax.fori_loop(0, count, block, 0)


def far_kernel(count, choice, last, h_ref, flag_ref, own_in, *refs):
    names = count if choice is None else count + 1
    parts, scores = [b.at[0] for b in refs[:names]], [b.at[1] for b in refs[:names]]
    sum_in, total_in, out_ref = refs[names : names + 3]
    refs = refs[names + 3 :]
    if not last:
        total_out = refs[0]
        refs = refs[1:]
    own_ref, x_buf, s_buf, own_square, total, sems, sum_sems = refs
    rows, knots = own_ref.shape
    own_copy = pltpu.make_async_copy(own_in.at[0], own_ref, sum_sems.at[2])
    own_copy.start()
    scale, rate = 2.0 / h_ref[0], LOG2E / h_ref[0]

    def part_copy(b, source):
        return pltpu.make_async_copy(source, x_buf.at[b], sems.at[b, 0])

    def score_copy(b, source):
        return pltpu.make_async_copy(source, s_buf.at[b], sems.at[b, 1])

    sums = (
        pltpu.make_async_copy(sum_in, out_ref, sum_sems.at[0]),
        pltpu.make_async_copy(total_in, total, sum_sems.at[1]),
    )
    for b in range(count):
        if b == choice:
            for value, n in enumerate((b, count)):
                for copy in (part_copy(b, parts[n]), score_copy(b, scores[n])):
                    pl.when((flag_ref[0] != 0) == bool(value))(copy.start)
        else:
            part_copy(b, parts[b]).start()
            score_copy(b, scores[b]).start()
        if b == 0:
            for copy in sums:
                copy.start()

    own_copy.wait()
    prepare_rows(own_ref, own_square, rate, 256)
    for copy in sums:
        copy.wait()

    def block(b, carry):
        part_copy(b, parts[0]).wait()
        score_copy(b, scores[0]).wait()
        x = x_buf[b].astype(jnp.float32)
        drift = (s_buf[b].astype(jnp.float32) - scale * x).astype(jnp.bfloat16)
        square = jnp.sum(jnp.transpose(fold(x * x)), axis=0, keepdims=True) * rate
        products = lax.dot_general(
            own_ref[...], x_buf[b], PRODUCT, preferred_element_type=jnp.float32
        )
        mine = jnp.concatenate([own_square[...]] * (rows // 128), axis=1)
        kernel = jnp.exp2(products * (2.0 * rate) - (mine + square))
        total[...] += fold(kernel)
        out_ref[...] += jnp.dot(
            kernel.astype(jnp.bfloat16), drift, preferred_element_type=jnp.float32
        )
        return carry

    lax.fori_loop(0, count, block, 0)

    def finish(t, carry):
        at = pl.ds(pl.multiple_of(t * 256, 256), 256)
        if last:
            mine = own_ref[at, :].astype(jnp.float32)
            out_ref[at, :] += scale * mine * jnp.sum(total[at, :], axis=1, keepdims=True)
        else:
            total_out[at, :] = total[at, :]
        return carry

    lax.fori_loop(0, rows // 256, finish, 0)


SMEM = pl.BlockSpec(memory_space=pltpu.SMEM)
VMEM = pl.BlockSpec(memory_space=pltpu.VMEM)
ANY = pl.BlockSpec(memory_space=pl.ANY)


def common(count, rows, knots, mebibytes):
    return dict(
        cost_estimate=pl.CostEstimate(
            flops=4 * count * rows * rows * knots,
            bytes_accessed=4 * (count + 2) * rows * knots,
            transcendentals=count * rows * rows,
        ),
        compiler_params=pltpu.CompilerParams(vmem_limit_bytes=mebibytes * 1024 * 1024),
    )


def near_terms(spread, own, blocks):
    rows, knots = own.shape[1:]
    count = len(blocks)
    return pl.pallas_call(
        functools.partial(near_kernel, count),
        out_shape=[
            jax.ShapeDtypeStruct((rows, knots), jnp.float32),
            jax.ShapeDtypeStruct((rows, 128), jnp.float32),
        ],
        in_specs=[SMEM] + [ANY] * (1 + count),
        out_specs=[VMEM, VMEM],
        scratch_shapes=[
            pltpu.VMEM((rows, knots), jnp.bfloat16),
            pltpu.VMEM((count, rows, knots), jnp.bfloat16),
            pltpu.VMEM((count, rows, knots), jnp.bfloat16),
            pltpu.VMEM((rows, 128), jnp.float32),
            pltpu.VMEM((8, rows), jnp.float32),
            pltpu.SemaphoreType.DMA((count, 2)),
            pltpu.SemaphoreType.DMA,
        ],
        **common(count, rows, knots, 14),
    )(spread, own, *blocks)


def far_terms(spread, flag, own, blocks, running, last, choice=None, other=None):
    rows, knots = own.shape[1:]
    count = len(blocks)
    operands = blocks + ([] if choice is None else [other])
    out_shape = [jax.ShapeDtypeStruct((rows, knots), jnp.float32)]
    if not last:
        out_shape.append(jax.ShapeDtypeStruct((rows, 128), jnp.float32))
    return pl.pallas_call(
        functools.partial(far_kernel, count, choice, last),
        out_shape=out_shape,
        in_specs=[SMEM, SMEM] + [ANY] * (len(operands) + 3),
        out_specs=[VMEM] * len(out_shape),
        scratch_shapes=[
            pltpu.VMEM((rows, knots), jnp.bfloat16),
            pltpu.VMEM((count, rows, knots), jnp.bfloat16),
            pltpu.VMEM((count, rows, knots), jnp.bfloat16),
            pltpu.VMEM((rows, 128), jnp.float32),
            pltpu.VMEM((rows, 128), jnp.float32),
            pltpu.SemaphoreType.DMA((count, 2)),
            pltpu.SemaphoreType.DMA((3,)),
        ],
        **common(count, rows, knots, 13 + 4 * count),
    )(spread, flag, own, *operands, *running)


def hop(block, move, pb_move=0):
    bits = move * lax.axis_size("pb") + pb_move
    if bits == 0:
        return block
    count = lax.axis_size(("pa", "pb"))
    return lax.ppermute(block, ("pa", "pb"), [(i, i ^ bits) for i in range(count)])


def route_kernel(plan_ref, low_move, high_move, high_y, both_y):
    one, two = plan_ref[0, 0], plan_ref[1, 0]
    swap = (one ^ 15) > (two ^ 15)
    low, high = jnp.where(swap, two, one), jnp.where(swap, one, two)
    low_move[0], high_move[0] = low & 15, high & 15
    high_y[0], both_y[0] = high >> 4, low >> 4


def route(plan):
    smem = pl.BlockSpec(memory_space=pltpu.SMEM)
    return pl.pallas_call(
        route_kernel,
        out_shape=[jax.ShapeDtypeStruct((1,), jnp.int32)] * 4,
        in_specs=[smem],
        out_specs=[smem] * 4,
    )(plan)


def per_device(particles, scores, spread, plan):
    own = jnp.stack([particles, scores])
    near_y = hop(own, Y_NEXT)
    mate = hop(own, 0, 1)
    low_move, high_move, high_y, both_y = route(plan)

    def low_exchange(move, spread, own, mate):
        return hop(own, move), near_terms(spread, own, [own, mate])

    low, running = lax.switch(
        low_move[0] - 1,
        [functools.partial(low_exchange, move) for move in range(1, PLANE)],
        *(spread, own, mate),
    )

    late_y, low = lax.optimization_barrier((near_y, low))
    far = hop(late_y, Y_NEXT, 2)
    low_y = hop(low, Y_NEXT)

    def stay(x, y):
        return jnp.where(high_move[0] >= 0, x, y)

    high = lax.switch(
        high_move[0],
        [stay] + [lambda x, y, move=move: hop(x, move) for move in range(1, PLANE)],
        *(jnp.where(high_y[0] == 1, near_y, own), own),
    )

    far, high = lax.optimization_barrier((far, high))
    far_mate = hop(far, 0, 1)
    running = far_terms(
        spread, both_y, own, [low, high], running, last=False, choice=0, other=low_y
    )
    return far_terms(spread, both_y, own, [far, far_mate], running, last=True)[0]


def solution(mesh):
    in_specs = (P(("pa", "pb"), None), P(("pa", "pb"), None), P(), P())
    out_specs = P(("pa", "pb"), None)
    return jax.shard_map(
        per_device, mesh=mesh, in_specs=in_specs, out_specs=out_specs, check_vma=False
    )
```

```python
import functools

import jax
import jax.numpy as jnp
from jax import lax
from jax.experimental import pallas as pl
from jax.experimental.pallas import tpu as pltpu
from jax.sharding import PartitionSpec as P

LOG2E = 1.4426950408889634
Y_NEXT = 16
PLANE = 16
PRODUCT = (((1,), (1,)), ((), ()))


def fold(square):
    total = square[:, :128]
    for i in range(128, square.shape[1], 128):
        total = total + square[:, i : i + 128]
    return total


def prepare_rows(own_ref, own_square, rate, step, also=None):
    def rows(t, carry):
        at = pl.ds(pl.multiple_of(t * step, step), step)
        mine = own_ref[at, :].astype(jnp.float32)
        square = jnp.sum(fold(mine * mine), axis=1, keepdims=True) * rate
        own_square[at, :] = jnp.broadcast_to(square, (step, 128))
        if also is not None:
            also(at)
        return carry

    lax.fori_loop(0, own_ref.shape[0] // step, rows, 0)


def near_kernel(count, h_ref, skip_ref, own_in, *refs):
    parts, scores = [b.at[0] for b in refs[:count]], [b.at[1] for b in refs[:count]]
    out_ref, total, own_ref, x_buf, d_buf, own_square, col_square, sems, own_sem = refs[count:]
    rows, knots = own_ref.shape
    own_copy = pltpu.make_async_copy(own_in.at[0], own_ref, own_sem)
    own_copy.start()
    scale, rate = 2.0 / h_ref[0], LOG2E / h_ref[0]
    step, tile = 32, 256

    def copies(b):
        return (
            pltpu.make_async_copy(parts[b], x_buf.at[b], sems.at[b, 0]),
            pltpu.make_async_copy(scores[b], d_buf.at[b], sems.at[b, 1]),
        )

    for b in range(count):
        for copy in copies(b):
            copy.start()

    def clear(at):
        out_ref[at, :] = jnp.zeros((step, knots), jnp.float32)
        total[at, :] = jnp.zeros((step, 128), jnp.float32)

    own_copy.wait()
    prepare_rows(own_ref, own_square, rate, step, clear)
    for b in range(count):
        for copy in copies(b):
            copy.wait()

    def block(b, carry):
        def columns(t, carry):
            squares = []
            for u in range(0, 128, step):
                at = pl.ds(pl.multiple_of(t * 128 + u, step), step)
                x = x_buf[b, at, :].astype(jnp.float32)
                d = d_buf[b, at, :].astype(jnp.float32) - scale * x
                d_buf[b, at, :] = d.astype(jnp.bfloat16)
                squares.append(fold(x * x))
            square = jnp.sum(jnp.transpose(jnp.concatenate(squares, axis=0)), axis=0, keepdims=True)
            at = pl.ds(pl.multiple_of(t * 128, 128), 128)
            col_square[:, at] = jnp.broadcast_to(square * rate, (8, 128))
            return carry

        lax.fori_loop(0, rows // 128, columns, 0)

        def one(t, carry):
            at = pl.ds(pl.multiple_of(t // (rows // tile) * tile, tile), tile)
            to = pl.ds(pl.multiple_of(t % (rows // tile) * tile, tile), tile)
            products = lax.dot_general(
                own_ref[at, :], x_buf[b, to, :], PRODUCT, preferred_element_type=jnp.float32
            )
            mine = jnp.concatenate([own_square[at, :]] * (tile // 128), axis=1)
            kernel = jnp.exp2(products * (2.0 * rate) - (mine + col_square[:1, to]))
            total[at, :] += fold(kernel)
            out_ref[at, :] += jnp.dot(
                kernel.astype(jnp.bfloat16), d_buf[b, to, :], preferred_element_type=jnp.float32
            )
            return carry

        lax.fori_loop(0, (rows // tile) ** 2, one, 0)
        return carry

    lax.fori_loop(0, count - skip_ref[0], block, 0)


def far_kernel(count, optional, last, h_ref, flag_ref, own_in, *refs):
    parts, scores = [b.at[0] for b in refs[:count]], [b.at[1] for b in refs[:count]]
    sum_in, total_in, result = refs[count : count + 3]
    refs = refs[count + 3 :]
    if last:
        out_ref, refs = refs[0], refs[1:]
    else:
        out_ref = result
    begin = 1 - flag_ref[0] if optional else 0
    if not last:
        total_out = refs[0]
        refs = refs[1:]
    own_ref, x_buf, s_buf, own_square, total, sems, sum_sems = refs
    rows, knots = own_ref.shape
    own_copy = pltpu.make_async_copy(own_in.at[0], own_ref, sum_sems.at[2])
    own_copy.start()
    scale, rate = 2.0 / h_ref[0], LOG2E / h_ref[0]

    def part_copy(b, source):
        return pltpu.make_async_copy(source, x_buf.at[b], sems.at[b, 0])

    def score_copy(b, source):
        return pltpu.make_async_copy(source, s_buf.at[b], sems.at[b, 1])

    sums = (
        pltpu.make_async_copy(sum_in, out_ref, sum_sems.at[0]),
        pltpu.make_async_copy(total_in, total, sum_sems.at[1]),
    )
    for copy in sums:
        copy.start()
    for b in range(count):
        for copy in (part_copy(b, parts[b]), score_copy(b, scores[b])):
            pl.when(begin <= b)(copy.start)

    own_copy.wait()
    prepare_rows(own_ref, own_square, rate, 256)
    for copy in sums:
        copy.wait()

    def block(b, carry):
        part_copy(b, parts[0]).wait()
        score_copy(b, scores[0]).wait()
        x = x_buf[b].astype(jnp.float32)
        drift = (s_buf[b].astype(jnp.float32) - scale * x).astype(jnp.bfloat16)
        square = jnp.sum(jnp.transpose(fold(x * x)), axis=0, keepdims=True) * rate
        products = lax.dot_general(
            own_ref[...], x_buf[b], PRODUCT, preferred_element_type=jnp.float32
        )
        mine = jnp.concatenate([own_square[...]] * (rows // 128), axis=1)
        kernel = jnp.exp2(products * (2.0 * rate) - (mine + square))
        total[...] += fold(kernel)
        out_ref[...] += jnp.dot(
            kernel.astype(jnp.bfloat16), drift, preferred_element_type=jnp.float32
        )
        return carry

    lax.fori_loop(begin, count, block, 0)

    def leave(t):
        at = pl.ds(pl.multiple_of(t * 256, 256), 256)
        return pltpu.make_async_copy(out_ref.at[at], result.at[at], sum_sems.at[3 + t])

    def finish(t, carry):
        at = pl.ds(pl.multiple_of(t * 256, 256), 256)
        if last:
            mine = own_ref[at, :].astype(jnp.float32)
            out_ref[at, :] += scale * mine * jnp.sum(total[at, :], axis=1, keepdims=True)
            leave(t).start()
        else:
            total_out[at, :] = total[at, :]
        return carry

    lax.fori_loop(0, rows // 256, finish, 0)
    if last:
        for t in range(rows // 256):
            leave(t).wait()


SMEM = pl.BlockSpec(memory_space=pltpu.SMEM)
VMEM = pl.BlockSpec(memory_space=pltpu.VMEM)
ANY = pl.BlockSpec(memory_space=pl.ANY)


def common(count, rows, knots, mebibytes):
    return dict(
        cost_estimate=pl.CostEstimate(
            flops=4 * count * rows * rows * knots,
            bytes_accessed=4 * (count + 2) * rows * knots,
            transcendentals=count * rows * rows,
        ),
        compiler_params=pltpu.CompilerParams(vmem_limit_bytes=mebibytes * 1024 * 1024),
    )


def near_terms(spread, skip, own, blocks):
    rows, knots = own.shape[1:]
    count = len(blocks)
    return pl.pallas_call(
        functools.partial(near_kernel, count),
        out_shape=[
            jax.ShapeDtypeStruct((rows, knots), jnp.float32),
            jax.ShapeDtypeStruct((rows, 128), jnp.float32),
        ],
        in_specs=[SMEM, SMEM] + [ANY] * (1 + count),
        out_specs=[VMEM, VMEM],
        scratch_shapes=[
            pltpu.VMEM((rows, knots), jnp.bfloat16),
            pltpu.VMEM((count, rows, knots), jnp.bfloat16),
            pltpu.VMEM((count, rows, knots), jnp.bfloat16),
            pltpu.VMEM((rows, 128), jnp.float32),
            pltpu.VMEM((8, rows), jnp.float32),
            pltpu.SemaphoreType.DMA((count, 2)),
            pltpu.SemaphoreType.DMA,
        ],
        **common(count, rows, knots, 18),
    )(spread, skip, own, *blocks)


def far_terms(spread, flag, own, blocks, running, last, optional=False):
    rows, knots = own.shape[1:]
    count = len(blocks)
    out_shape = [jax.ShapeDtypeStruct((rows, knots), jnp.float32)]
    if not last:
        out_shape.append(jax.ShapeDtypeStruct((rows, 128), jnp.float32))
    return pl.pallas_call(
        functools.partial(far_kernel, count, optional, last),
        out_shape=out_shape,
        in_specs=[SMEM, SMEM] + [ANY] * (count + 3),
        out_specs=[ANY] if last else [VMEM] * 2,
        scratch_shapes=([pltpu.VMEM((rows, knots), jnp.float32)] if last else [])
        + [
            pltpu.VMEM((rows, knots), jnp.bfloat16),
            pltpu.VMEM((count, rows, knots), jnp.bfloat16),
            pltpu.VMEM((count, rows, knots), jnp.bfloat16),
            pltpu.VMEM((rows, 128), jnp.float32),
            pltpu.VMEM((rows, 128), jnp.float32),
            pltpu.SemaphoreType.DMA((count, 2)),
            pltpu.SemaphoreType.DMA((3 + rows // 256,)),
        ],
        **common(count, rows, knots, (17 if last else 13) + 4 * count),
    )(spread, flag, own, *blocks, *running)


def hop(block, move, pb_move=0):
    bits = move * lax.axis_size("pb") + pb_move
    if bits == 0:
        return block
    count = lax.axis_size(("pa", "pb"))
    return lax.ppermute(block, ("pa", "pb"), [(i, i ^ bits) for i in range(count)])


def begin_kernel(plan, particles, scores, out, low_move, high_move, high_y, both_y, sems):
    copies = [
        pltpu.make_async_copy(source, out.at[n], sems.at[n])
        for n, source in enumerate((particles, scores))
    ]
    for copy in copies:
        copy.start()
    one, two = plan[0, 0], plan[1, 0]
    swap = (one ^ 15) > (two ^ 15)
    low, high = jnp.where(swap, two, one), jnp.where(swap, one, two)
    low_move[0], high_move[0] = low & 15, high & 15
    high_y[0], both_y[0] = high >> 4, low >> 4
    for copy in copies:
        copy.wait()


def begin(particles, scores, plan):
    return pl.pallas_call(
        begin_kernel,
        out_shape=[jax.ShapeDtypeStruct((2, *particles.shape), particles.dtype)]
        + [jax.ShapeDtypeStruct((1,), jnp.int32)] * 4,
        in_specs=[SMEM, ANY, ANY],
        out_specs=[VMEM] + [SMEM] * 4,
        scratch_shapes=[pltpu.SemaphoreType.DMA((2,))],
    )(plan, particles, scores)


def per_device(particles, scores, spread, plan):
    own, low_move, high_move, high_y, both_y = begin(particles, scores, plan)
    near_y = hop(own, Y_NEXT)

    low = lax.switch(
        low_move[0] - 1, [functools.partial(hop, move=move) for move in range(1, PLANE)], own
    )

    late_y, late_own, low = lax.optimization_barrier((near_y, own, low))
    far = hop(late_y, Y_NEXT, 2)
    low_y = hop(low, Y_NEXT)
    mate = hop(own, 0, 1)
    start = jnp.where(high_y[0] == 1, near_y, own)

    def high_exchange(move, start, spread, both_y, own, mate, low):
        near = near_terms(spread, both_y, own, [own, mate, low])
        moved = hop(start, move) if move else jnp.where(both_y[0] >= 0, start, own)
        return moved, near

    high, running = lax.switch(
        high_move[0],
        [functools.partial(high_exchange, move) for move in range(PLANE)],
        *(start, spread, both_y, own, mate, low),
    )

    far, high = lax.optimization_barrier((far, high))
    far_mate = hop(far, 0, 1)
    running = far_terms(
        spread, both_y, own, [low_y, high, far], running, last=False, optional=True
    )
    return far_terms(spread, both_y, own, [far_mate], running, last=True)[0]


def solution(mesh):
    in_specs = (P(("pa", "pb"), None), P(("pa", "pb"), None), P(), P())
    out_specs = P(("pa", "pb"), None)
    return jax.shard_map(
        per_device, mesh=mesh, in_specs=in_specs, out_specs=out_specs, check_vma=False
    )
```

```python
import functools

import jax
import jax.numpy as jnp
from jax import lax
from jax.experimental import pallas as pl
from jax.experimental.pallas import tpu as pltpu
from jax.sharding import PartitionSpec as P

LOG2E = 1.4426950408889634
Y_NEXT = 16
PLANE = 16
PRODUCT = (((1,), (1,)), ((), ()))


def fold(square):
    total = square[:, :128]
    for i in range(128, square.shape[1], 128):
        total = total + square[:, i : i + 128]
    return total


def prepare_rows(own_ref, own_square, rate, step, also=None):
    def rows(t, carry):
        at = pl.ds(pl.multiple_of(t * step, step), step)
        mine = own_ref[at, :].astype(jnp.float32)
        square = jnp.sum(fold(mine * mine), axis=1, keepdims=True) * rate
        own_square[at, :] = jnp.broadcast_to(square, (step, 128))
        if also is not None:
            also(at)
        return carry

    lax.fori_loop(0, own_ref.shape[0] // step, rows, 0)


def near_kernel(count, h_ref, skip_ref, own_in, *refs):
    parts, scores = [b.at[0] for b in refs[:count]], [b.at[1] for b in refs[:count]]
    out_ref, total, own_square, own_ref, x_buf, d_buf, col_square, sems, own_sem = refs[count:]
    rows, knots = own_ref.shape
    own_copy = pltpu.make_async_copy(own_in.at[0], own_ref, own_sem)
    own_copy.start()
    scale, rate = 2.0 / h_ref[0], LOG2E / h_ref[0]
    step, tile = 32, 256

    def copies(b):
        return (
            pltpu.make_async_copy(parts[b], x_buf.at[b], sems.at[b, 0]),
            pltpu.make_async_copy(scores[b], d_buf.at[b], sems.at[b, 1]),
        )

    for b in range(count):
        for copy in copies(b):
            copy.start()

    def clear(at):
        out_ref[at, :] = jnp.zeros((step, knots), jnp.float32)
        total[at, :] = jnp.zeros((step, 128), jnp.float32)

    own_copy.wait()
    prepare_rows(own_ref, own_square, rate, step, clear)
    for b in range(count):
        for copy in copies(b):
            copy.wait()

    def block(b, carry):
        def columns(t, carry):
            squares = []
            for u in range(0, 128, step):
                at = pl.ds(pl.multiple_of(t * 128 + u, step), step)
                x = x_buf[b, at, :].astype(jnp.float32)
                d = d_buf[b, at, :].astype(jnp.float32) - scale * x
                d_buf[b, at, :] = d.astype(jnp.bfloat16)
                squares.append(fold(x * x))
            square = jnp.sum(jnp.transpose(jnp.concatenate(squares, axis=0)), axis=0, keepdims=True)
            at = pl.ds(pl.multiple_of(t * 128, 128), 128)
            col_square[:, at] = jnp.broadcast_to(square * rate, (8, 128))
            return carry

        lax.fori_loop(0, rows // 128, columns, 0)

        def one(t, carry):
            at = pl.ds(pl.multiple_of(t // (rows // tile) * tile, tile), tile)
            to = pl.ds(pl.multiple_of(t % (rows // tile) * tile, tile), tile)
            products = lax.dot_general(
                own_ref[at, :], x_buf[b, to, :], PRODUCT, preferred_element_type=jnp.float32
            )
            mine = jnp.concatenate([own_square[at, :]] * (tile // 128), axis=1)
            kernel = jnp.exp2(products * (2.0 * rate) - (mine + col_square[:1, to]))
            total[at, :] += fold(kernel)
            out_ref[at, :] += jnp.dot(
                kernel.astype(jnp.bfloat16), d_buf[b, to, :], preferred_element_type=jnp.float32
            )
            return carry

        lax.fori_loop(0, (rows // tile) ** 2, one, 0)
        return carry

    lax.fori_loop(0, count - skip_ref[0], block, 0)


def far_kernel(count, optional, last, h_ref, flag_ref, own_in, *refs):
    parts, scores = [b.at[0] for b in refs[:count]], [b.at[1] for b in refs[:count]]
    square_in, sum_in, total_in, result = refs[count : count + 4]
    refs = refs[count + 4 :]
    if last:
        out_ref, refs = refs[0], refs[1:]
    else:
        out_ref = result
    begin = 1 - flag_ref[0] if optional else 0
    if not last:
        total_out = refs[0]
        refs = refs[1:]
    own_ref, x_buf, s_buf, own_square, total, sems, sum_sems = refs
    rows, knots = own_ref.shape
    own_copy = pltpu.make_async_copy(own_in.at[0], own_ref, sum_sems.at[2])
    own_copy.start()
    scale, rate = 2.0 / h_ref[0], LOG2E / h_ref[0]

    def part_copy(b, source):
        return pltpu.make_async_copy(source, x_buf.at[b], sems.at[b, 0])

    def score_copy(b, source):
        return pltpu.make_async_copy(source, s_buf.at[b], sems.at[b, 1])

    sums = (
        pltpu.make_async_copy(sum_in, out_ref, sum_sems.at[0]),
        pltpu.make_async_copy(total_in, total, sum_sems.at[1]),
        pltpu.make_async_copy(square_in, own_square, sum_sems.at[3]),
    )
    for copy in sums:
        copy.start()
    for b in range(count):
        for copy in (part_copy(b, parts[b]), score_copy(b, scores[b])):
            pl.when(begin <= b)(copy.start)

    own_copy.wait()
    for copy in sums:
        copy.wait()

    def block(b, carry):
        part_copy(b, parts[0]).wait()
        score_copy(b, scores[0]).wait()
        x = x_buf[b].astype(jnp.float32)
        drift = (s_buf[b].astype(jnp.float32) - scale * x).astype(jnp.bfloat16)
        square = jnp.sum(jnp.transpose(fold(x * x)), axis=0, keepdims=True) * rate
        products = lax.dot_general(
            own_ref[...], x_buf[b], PRODUCT, preferred_element_type=jnp.float32
        )
        mine = jnp.concatenate([own_square[...]] * (rows // 128), axis=1)
        kernel = jnp.exp2(products * (2.0 * rate) - (mine + square))
        total[...] += fold(kernel)
        out_ref[...] += jnp.dot(
            kernel.astype(jnp.bfloat16), drift, preferred_element_type=jnp.float32
        )
        return carry

    lax.fori_loop(begin, count, block, 0)

    def leave(t):
        at = pl.ds(pl.multiple_of(t * 256, 256), 256)
        return pltpu.make_async_copy(out_ref.at[at], result.at[at], sum_sems.at[4 + t])

    def finish(t, carry):
        at = pl.ds(pl.multiple_of(t * 256, 256), 256)
        if last:
            mine = own_ref[at, :].astype(jnp.float32)
            out_ref[at, :] += scale * mine * jnp.sum(total[at, :], axis=1, keepdims=True)
            leave(t).start()
        else:
            total_out[at, :] = total[at, :]
        return carry

    lax.fori_loop(0, rows // 256, finish, 0)
    if last:
        for t in range(rows // 256):
            leave(t).wait()


SMEM = pl.BlockSpec(memory_space=pltpu.SMEM)
VMEM = pl.BlockSpec(memory_space=pltpu.VMEM)
ANY = pl.BlockSpec(memory_space=pl.ANY)


def common(count, rows, knots, mebibytes):
    return dict(
        cost_estimate=pl.CostEstimate(
            flops=4 * count * rows * rows * knots,
            bytes_accessed=4 * (count + 2) * rows * knots,
            transcendentals=count * rows * rows,
        ),
        compiler_params=pltpu.CompilerParams(vmem_limit_bytes=mebibytes * 1024 * 1024),
    )


def near_terms(spread, skip, own, blocks):
    rows, knots = own.shape[1:]
    count = len(blocks)
    return pl.pallas_call(
        functools.partial(near_kernel, count),
        out_shape=[
            jax.ShapeDtypeStruct((rows, knots), jnp.float32),
            jax.ShapeDtypeStruct((rows, 128), jnp.float32),
            jax.ShapeDtypeStruct((rows, 128), jnp.float32),
        ],
        in_specs=[SMEM, SMEM] + [ANY] * (1 + count),
        out_specs=[VMEM] * 3,
        scratch_shapes=[
            pltpu.VMEM((rows, knots), jnp.bfloat16),
            pltpu.VMEM((count, rows, knots), jnp.bfloat16),
            pltpu.VMEM((count, rows, knots), jnp.bfloat16),
            pltpu.VMEM((8, rows), jnp.float32),
            pltpu.SemaphoreType.DMA((count, 2)),
            pltpu.SemaphoreType.DMA,
        ],
        **common(count, rows, knots, 18),
    )(spread, skip, own, *blocks)


def far_terms(spread, flag, own, own_square, blocks, running, last, optional=False):
    rows, knots = own.shape[1:]
    count = len(blocks)
    out_shape = [jax.ShapeDtypeStruct((rows, knots), jnp.float32)]
    if not last:
        out_shape.append(jax.ShapeDtypeStruct((rows, 128), jnp.float32))
    return pl.pallas_call(
        functools.partial(far_kernel, count, optional, last),
        out_shape=out_shape,
        in_specs=[SMEM, SMEM] + [ANY] * (count + 4),
        out_specs=[ANY] if last else [VMEM] * 2,
        scratch_shapes=([pltpu.VMEM((rows, knots), jnp.float32)] if last else [])
        + [
            pltpu.VMEM((rows, knots), jnp.bfloat16),
            pltpu.VMEM((count, rows, knots), jnp.bfloat16),
            pltpu.VMEM((count, rows, knots), jnp.bfloat16),
            pltpu.VMEM((rows, 128), jnp.float32),
            pltpu.VMEM((rows, 128), jnp.float32),
            pltpu.SemaphoreType.DMA((count, 2)),
            pltpu.SemaphoreType.DMA((4 + rows // 256,)),
        ],
        **common(count, rows, knots, (17 if last else 13) + 4 * count),
    )(spread, flag, own, *blocks, own_square, *running)


def hop(block, move, pb_move=0):
    bits = move * lax.axis_size("pb") + pb_move
    if bits == 0:
        return block
    count = lax.axis_size(("pa", "pb"))
    return lax.ppermute(block, ("pa", "pb"), [(i, i ^ bits) for i in range(count)])


def begin_kernel(plan, particles, scores, out, low_move, high_move, high_y, both_y, sems):
    copies = [
        pltpu.make_async_copy(source, out.at[n], sems.at[n])
        for n, source in enumerate((particles, scores))
    ]
    for copy in copies:
        copy.start()
    one, two = plan[0, 0], plan[1, 0]
    swap = (one ^ 15) > (two ^ 15)
    low, high = jnp.where(swap, two, one), jnp.where(swap, one, two)
    low_move[0], high_move[0] = low & 15, high & 15
    high_y[0], both_y[0] = high >> 4, low >> 4
    for copy in copies:
        copy.wait()


def begin(particles, scores, plan):
    return pl.pallas_call(
        begin_kernel,
        out_shape=[jax.ShapeDtypeStruct((2, *particles.shape), particles.dtype)]
        + [jax.ShapeDtypeStruct((1,), jnp.int32)] * 4,
        in_specs=[SMEM, ANY, ANY],
        out_specs=[VMEM] + [SMEM] * 4,
        scratch_shapes=[pltpu.SemaphoreType.DMA((2,))],
    )(plan, particles, scores)


def per_device(particles, scores, spread, plan):
    own, low_move, high_move, high_y, both_y = begin(particles, scores, plan)
    near_y = hop(own, Y_NEXT)

    low = lax.switch(
        low_move[0] - 1, [functools.partial(hop, move=move) for move in range(1, PLANE)], own
    )

    late_y, late_own, low = lax.optimization_barrier((near_y, own, low))
    far = hop(late_y, Y_NEXT, 2)
    low_y = hop(low, Y_NEXT)
    mate = hop(own, 0, 1)
    start = jnp.where(high_y[0] == 1, near_y, own)

    def high_exchange(move, start, spread, both_y, own, mate, low):
        near = near_terms(spread, both_y, own, [own, mate, low])
        moved = hop(start, move) if move else jnp.where(both_y[0] >= 0, start, own)
        return moved, near

    high, (*running, own_square) = lax.switch(
        high_move[0],
        [functools.partial(high_exchange, move) for move in range(PLANE)],
        *(start, spread, both_y, own, mate, low),
    )

    far, high = lax.optimization_barrier((far, high))
    far_mate = hop(far, 0, 1)
    running = far_terms(
        spread, both_y, own, own_square, [low_y, high, far], running, last=False, optional=True
    )
    return far_terms(spread, both_y, own, own_square, [far_mate], running, last=True)[0]


def solution(mesh):
    in_specs = (P(("pa", "pb"), None), P(("pa", "pb"), None), P(), P())
    out_specs = P(("pa", "pb"), None)
    return jax.shard_map(
        per_device, mesh=mesh, in_specs=in_specs, out_specs=out_specs, check_vma=False
    )
```

```python
import functools

import jax
import jax.numpy as jnp
from jax import lax
from jax.experimental import pallas as pl
from jax.experimental.pallas import tpu as pltpu
from jax.sharding import PartitionSpec as P

LOG2E = 1.4426950408889634
Y_NEXT = 16
PLANE = 16
PRODUCT = (((1,), (1,)), ((), ()))


def fold(square):
    total = square[:, :128]
    for i in range(128, square.shape[1], 128):
        total = total + square[:, i : i + 128]
    return total


def prepare_rows(own_ref, own_square, rate, step, also=None):
    def rows(t, carry):
        at = pl.ds(pl.multiple_of(t * step, step), step)
        mine = own_ref[at, :].astype(jnp.float32)
        square = jnp.sum(fold(mine * mine), axis=1, keepdims=True) * rate
        own_square[at, :] = jnp.broadcast_to(square, (step, 128))
        if also is not None:
            also(at)
        return carry

    lax.fori_loop(0, own_ref.shape[0] // step, rows, 0)


def near_kernel(count, h_ref, skip_ref, own_in, *refs):
    parts, scores = [b.at[0] for b in refs[:count]], [b.at[1] for b in refs[:count]]
    out_ref, total, own_square, own_ref, x_buf, d_buf, col_square, sems, own_sem = refs[count:]
    rows, knots = own_ref.shape
    own_copy = pltpu.make_async_copy(own_in.at[0], own_ref, own_sem)
    own_copy.start()
    scale, rate = 2.0 / h_ref[0], LOG2E / h_ref[0]
    step, tile = 32, 256

    def copies(b):
        return (
            pltpu.make_async_copy(parts[b], x_buf.at[b], sems.at[b, 0]),
            pltpu.make_async_copy(scores[b], d_buf.at[b], sems.at[b, 1]),
        )

    for b in range(count):
        for copy in copies(b):
            copy.start()

    def clear(at):
        out_ref[at, :] = jnp.zeros((step, knots), jnp.float32)
        total[at, :] = jnp.zeros((step, 128), jnp.float32)

    own_copy.wait()
    prepare_rows(own_ref, own_square, rate, step, clear)
    for b in range(count):
        for copy in copies(b):
            copy.wait()

    def block(b, carry):
        def columns(t, carry):
            squares = []
            for u in range(0, 128, step):
                at = pl.ds(pl.multiple_of(t * 128 + u, step), step)
                x = x_buf[b, at, :].astype(jnp.float32)
                d = d_buf[b, at, :].astype(jnp.float32) - scale * x
                d_buf[b, at, :] = d.astype(jnp.bfloat16)
                squares.append(fold(x * x))
            square = jnp.sum(jnp.transpose(jnp.concatenate(squares, axis=0)), axis=0, keepdims=True)
            at = pl.ds(pl.multiple_of(t * 128, 128), 128)
            col_square[:, at] = jnp.broadcast_to(square * rate, (8, 128))
            return carry

        lax.fori_loop(0, rows // 128, columns, 0)

        def one(t, carry):
            at = pl.ds(pl.multiple_of(t // (rows // tile) * tile, tile), tile)
            to = pl.ds(pl.multiple_of(t % (rows // tile) * tile, tile), tile)
            products = lax.dot_general(
                own_ref[at, :], x_buf[b, to, :], PRODUCT, preferred_element_type=jnp.float32
            )
            mine = jnp.concatenate([own_square[at, :]] * (tile // 128), axis=1)
            kernel = jnp.exp2(products * (2.0 * rate) - (mine + col_square[:1, to]))
            total[at, :] += fold(kernel)
            out_ref[at, :] += jnp.dot(
                kernel.astype(jnp.bfloat16), d_buf[b, to, :], preferred_element_type=jnp.float32
            )
            return carry

        lax.fori_loop(0, (rows // tile) ** 2, one, 0)
        return carry

    lax.fori_loop(0, count - skip_ref[0], block, 0)


def far_kernel(count, optional, last, h_ref, flag_ref, own_in, *refs):
    parts, scores = [b.at[0] for b in refs[:count]], [b.at[1] for b in refs[:count]]
    square_in, sum_in, total_in, result = refs[count : count + 4]
    refs = refs[count + 4 :]
    if last:
        out_ref, refs = refs[0], refs[1:]
    else:
        out_ref = result
    begin = 1 - flag_ref[0] if optional else 0
    if not last:
        total_out = refs[0]
        refs = refs[1:]
    own_ref, x_buf, s_buf, own_square, total, sems, sum_sems = refs
    rows, knots = own_ref.shape
    own_copy = pltpu.make_async_copy(own_in.at[0], own_ref, sum_sems.at[2])
    own_copy.start()
    scale, rate = 2.0 / h_ref[0], LOG2E / h_ref[0]

    def part_copy(b, source):
        return pltpu.make_async_copy(source, x_buf.at[b], sems.at[b, 0])

    def score_copy(b, source):
        return pltpu.make_async_copy(source, s_buf.at[b], sems.at[b, 1])

    drive_copy = pltpu.make_async_copy(sum_in, out_ref, sum_sems.at[0])
    sums = (
        pltpu.make_async_copy(total_in, total, sum_sems.at[1]),
        pltpu.make_async_copy(square_in, own_square, sum_sems.at[3]),
    )
    for copy in sums:
        copy.start()
    for b in range(count):
        for copy in (part_copy(b, parts[b]), score_copy(b, scores[b])):
            pl.when(begin <= b)(copy.start)
        if b == min(1, count - 1):
            drive_copy.start()

    own_copy.wait()
    for copy in sums:
        copy.wait()

    def block(b, carry):
        part_copy(b, parts[0]).wait()
        score_copy(b, scores[0]).wait()
        x = x_buf[b].astype(jnp.float32)
        drift = (s_buf[b].astype(jnp.float32) - scale * x).astype(jnp.bfloat16)
        square = jnp.sum(jnp.transpose(fold(x * x)), axis=0, keepdims=True) * rate
        products = lax.dot_general(
            own_ref[...], x_buf[b], PRODUCT, preferred_element_type=jnp.float32
        )
        mine = jnp.concatenate([own_square[...]] * (rows // 128), axis=1)
        kernel = jnp.exp2(products * (2.0 * rate) - (mine + square))
        total[...] += fold(kernel)
        pl.when(b == begin)(drive_copy.wait)
        out_ref[...] += jnp.dot(
            kernel.astype(jnp.bfloat16), drift, preferred_element_type=jnp.float32
        )
        return carry

    lax.fori_loop(begin, count, block, 0)

    def leave(t):
        at = pl.ds(pl.multiple_of(t * 256, 256), 256)
        return pltpu.make_async_copy(out_ref.at[at], result.at[at], sum_sems.at[4 + t])

    def finish(t, carry):
        at = pl.ds(pl.multiple_of(t * 256, 256), 256)
        if last:
            mine = own_ref[at, :].astype(jnp.float32)
            out_ref[at, :] += scale * mine * jnp.sum(total[at, :], axis=1, keepdims=True)
            leave(t).start()
        else:
            total_out[at, :] = total[at, :]
        return carry

    lax.fori_loop(0, rows // 256, finish, 0)
    if last:
        for t in range(rows // 256):
            leave(t).wait()


SMEM = pl.BlockSpec(memory_space=pltpu.SMEM)
VMEM = pl.BlockSpec(memory_space=pltpu.VMEM)
ANY = pl.BlockSpec(memory_space=pl.ANY)


def common(count, rows, knots, mebibytes):
    return dict(
        cost_estimate=pl.CostEstimate(
            flops=4 * count * rows * rows * knots,
            bytes_accessed=4 * (count + 2) * rows * knots,
            transcendentals=count * rows * rows,
        ),
        compiler_params=pltpu.CompilerParams(vmem_limit_bytes=mebibytes * 1024 * 1024),
    )


def near_terms(spread, skip, own, blocks):
    rows, knots = own.shape[1:]
    count = len(blocks)
    return pl.pallas_call(
        functools.partial(near_kernel, count),
        out_shape=[
            jax.ShapeDtypeStruct((rows, knots), jnp.float32),
            jax.ShapeDtypeStruct((rows, 128), jnp.float32),
            jax.ShapeDtypeStruct((rows, 128), jnp.float32),
        ],
        in_specs=[SMEM, SMEM] + [ANY] * (1 + count),
        out_specs=[VMEM] * 3,
        scratch_shapes=[
            pltpu.VMEM((rows, knots), jnp.bfloat16),
            pltpu.VMEM((count, rows, knots), jnp.bfloat16),
            pltpu.VMEM((count, rows, knots), jnp.bfloat16),
            pltpu.VMEM((8, rows), jnp.float32),
            pltpu.SemaphoreType.DMA((count, 2)),
            pltpu.SemaphoreType.DMA,
        ],
        **common(count, rows, knots, 18),
    )(spread, skip, own, *blocks)


def far_terms(spread, flag, own, own_square, blocks, running, last, optional=False):
    rows, knots = own.shape[1:]
    count = len(blocks)
    out_shape = [jax.ShapeDtypeStruct((rows, knots), jnp.float32)]
    if not last:
        out_shape.append(jax.ShapeDtypeStruct((rows, 128), jnp.float32))
    return pl.pallas_call(
        functools.partial(far_kernel, count, optional, last),
        out_shape=out_shape,
        in_specs=[SMEM, SMEM] + [ANY] * (count + 4),
        out_specs=[ANY] if last else [VMEM] * 2,
        scratch_shapes=([pltpu.VMEM((rows, knots), jnp.float32)] if last else [])
        + [
            pltpu.VMEM((rows, knots), jnp.bfloat16),
            pltpu.VMEM((count, rows, knots), jnp.bfloat16),
            pltpu.VMEM((count, rows, knots), jnp.bfloat16),
            pltpu.VMEM((rows, 128), jnp.float32),
            pltpu.VMEM((rows, 128), jnp.float32),
            pltpu.SemaphoreType.DMA((count, 2)),
            pltpu.SemaphoreType.DMA((4 + rows // 256,)),
        ],
        **common(count, rows, knots, (17 if last else 13) + 4 * count),
    )(spread, flag, own, *blocks, own_square, *running)


def hop(block, move, pb_move=0):
    bits = move * lax.axis_size("pb") + pb_move
    if bits == 0:
        return block
    count = lax.axis_size(("pa", "pb"))
    return lax.ppermute(block, ("pa", "pb"), [(i, i ^ bits) for i in range(count)])


def begin_kernel(plan, particles, scores, out, low_move, high_move, high_y, both_y, sems):
    copies = [
        pltpu.make_async_copy(source, out.at[n], sems.at[n])
        for n, source in enumerate((particles, scores))
    ]
    for copy in copies:
        copy.start()
    one, two = plan[0, 0], plan[1, 0]
    swap = (one ^ 15) > (two ^ 15)
    low, high = jnp.where(swap, two, one), jnp.where(swap, one, two)
    low_move[0], high_move[0] = low & 15, high & 15
    high_y[0], both_y[0] = high >> 4, low >> 4
    for copy in copies:
        copy.wait()


def begin(particles, scores, plan):
    return pl.pallas_call(
        begin_kernel,
        out_shape=[jax.ShapeDtypeStruct((2, *particles.shape), particles.dtype)]
        + [jax.ShapeDtypeStruct((1,), jnp.int32)] * 4,
        in_specs=[SMEM, ANY, ANY],
        out_specs=[VMEM] + [SMEM] * 4,
        scratch_shapes=[pltpu.SemaphoreType.DMA((2,))],
    )(plan, particles, scores)


def per_device(particles, scores, spread, plan):
    own, low_move, high_move, high_y, both_y = begin(particles, scores, plan)
    near_y = hop(own, Y_NEXT)

    low = lax.switch(
        low_move[0] - 1, [functools.partial(hop, move=move) for move in range(1, PLANE)], own
    )

    late_y, late_own, low = lax.optimization_barrier((near_y, own, low))
    far = hop(late_y, Y_NEXT, 2)
    low_y = hop(low, Y_NEXT)
    mate = hop(own, 0, 1)
    start = jnp.where(high_y[0] == 1, near_y, own)

    def high_exchange(move, start, spread, both_y, own, mate, low):
        near = near_terms(spread, both_y, own, [own, mate, low])
        moved = hop(start, move) if move else jnp.where(both_y[0] >= 0, start, own)
        return moved, near

    high, (*running, own_square) = lax.switch(
        high_move[0],
        [functools.partial(high_exchange, move) for move in range(PLANE)],
        *(start, spread, both_y, own, mate, low),
    )

    far, high = lax.optimization_barrier((far, high))
    far_mate = hop(far, 0, 1)
    running = far_terms(
        spread, both_y, own, own_square, [low_y, high, far], running, last=False, optional=True
    )
    return far_terms(spread, both_y, own, own_square, [far_mate], running, last=True)[0]


def solution(mesh):
    in_specs = (P(("pa", "pb"), None), P(("pa", "pb"), None), P(), P())
    out_specs = P(("pa", "pb"), None)
    return jax.shard_map(
        per_device, mesh=mesh, in_specs=in_specs, out_specs=out_specs, check_vma=False
    )
```
